32 devices in a mesh: clips: 2 (over y), patch: 4 (over z), span: 2 (over x), chan: 2 (over core).
Axes of the slice: x: 2, y: 2, z: 4, core: 2. Of those that a mesh axis runs over, the one named last changes fastest.
Arguments:
- latent_tiles: bfloat16 [4, 256, 4, 384], P(('clips', 'span'), 'patch'), parts along dimension 0, may hold values from -12 to 12
- route: int32 [4, 256], P(('clips', 'span')), parts along dimension 0, may hold values from 0 to 255, as said below
- w_query: bfloat16 [384, 384], replicated, may hold values from -0.5 to 4.6
- w_keyval: bfloat16 [384, 768], replicated, may hold values from -0.5 to 4.6
- conv_weight: bfloat16 [3, 3, 3, 384, 384], P(None, None, None, None, 'chan'), may hold values from -0.0625 to 0.0625
Outputs:
- decoded: bfloat16 [8, 8, 64, 384], P(('clips', 'span'), 'patch', None, 'chan'), parts along dimension 0
The draws below stay inside these ranges and needn't reach their ends.
There are 2 independent parts, one for each index of `clips`. The reference program is written for one: setup_inputs(seed, part) draws one part's arguments, and reference() takes and returns one part's arrays. A program takes and returns all parts, laid end to end along the dimension named above; an argument that names none is the same for every part. Nothing has to cross between parts.
Inputs may be any that keep to these rules, and one draw needn't show every extreme that they name: `route`: each span's row is a permutation of 0 .. 255. The 64 tiles of positions j * 64 to (j + 1) * 64 - 1 go to at most 32 per owner, and in every span some such group sends exactly 32 to one owner.
All inputs are finite; a program needn't handle non-finite values.
Results may differ from the reference program's by a relative error of at most 0.0065.
Values may be sent and summed in bfloat16 or wider, within the bound.
A program may use at most 64 MiB of HBM per device.

```python
import math
import jax
import jax.numpy as jnp
from jax import lax

C = 384
W = 64
RD = 2
FD = 2
TCELL = 4
SPANS = 2
FRAMES = 4
ROWS = 8
TPD = 64
TILES = 256


def route_block(key):
    patch_count = TILES // TPD
    per_device = TPD
    slot_count = 2 * per_device // patch_count
    keys_split = jax.random.split(key, 5)
    shift_order = jax.random.permutation(keys_split[0], patch_count).astype(jnp.int32)
    second = jax.random.randint(keys_split[1], (patch_count // 2,), 0, slot_count + 1)
    second = second.at[0].set(0)
    counts = jnp.zeros((patch_count,), jnp.int32)
    counts = counts.at[shift_order[0::2]].set(slot_count - second)
    counts = counts.at[shift_order[1::2]].set(second)
    bounds = jnp.cumsum(counts)
    positions = jnp.arange(per_device, dtype=jnp.int32)
    shift_list = jnp.sum((bounds[None, :] <= positions[:, None]).astype(jnp.int32), axis=1)
    owner_order = jax.random.permutation(keys_split[2], patch_count).astype(jnp.int32)
    sources = jnp.arange(patch_count, dtype=jnp.int32)
    destination = owner_order[(sources[:, None] + shift_list[None, :]) % patch_count]
    scores = jax.random.randint(keys_split[3], (patch_count, per_device), 0, 1 << 20) * per_device + positions[None, :]
    shuffle = jnp.argsort(scores, axis=1)
    owners = jnp.take_along_axis(destination, shuffle, axis=1).reshape(-1)
    priority = jax.random.permutation(keys_split[4], patch_count * per_device).astype(jnp.int32)
    same_owner = owners[:, None] == owners[None, :]
    before = priority[None, :] < priority[:, None]
    spot_ids = jnp.sum((same_owner & before).astype(jnp.int32), axis=1)
    return (owners * per_device + spot_ids).astype(jnp.int32)


def draw_route(key, part):
    return jax.vmap(route_block)(jax.random.split(key, SPANS))


def draw_latent_tiles(key, part):
    shape = (SPANS, TILES, TCELL, C)
    keys_split = jax.random.split(key, 1)
    values = jnp.clip(jax.random.normal(keys_split[0], shape, jnp.float32), -6.0, 6.0)
    return values.astype(jnp.bfloat16)


def draw_w_query(key, part):
    keys_split = jax.random.split(jax.random.fold_in(key, 11), 2)
    values = 0.08 * jnp.clip(jax.random.normal(keys_split[1], (C, C), jnp.float32), -6.0, 6.0)
    return values.astype(jnp.bfloat16)


def draw_w_keyval(key, part):
    keys_split = jax.random.split(jax.random.fold_in(key, 23), 3)
    values = 0.08 * jnp.clip(jax.random.normal(keys_split[2], (C, 2 * C), jnp.float32), -6.0, 6.0)
    return values.astype(jnp.bfloat16)


def shard_levels(own_key, dims, shards, low, top_value):
    def one(axis_at, blocks):
        draws = jax.random.uniform(jax.random.fold_in(jax.random.fold_in(own_key, 6), axis_at), (blocks,), jnp.float32, low / len(shards), top_value / len(shards))
        return jnp.repeat(jnp.exp(draws), dims[axis_at] // blocks).reshape((-1,) + (1,) * (len(dims) - axis_at - 1))

    level = one(*shards[0])
    for cut in shards[1:]:
        level = level * one(*cut)
    return level


def centred(key, dims, deviation, limit, pieces=(), kind=jnp.bfloat16):
    loudness = shard_levels(key, dims, pieces, -0.22, 0.18) if pieces else 1.0
    drawn = jax.random.normal(key, dims, jnp.float32) * deviation * loudness
    return jnp.minimum(jnp.maximum(drawn, -limit), limit).astype(kind)


def setup_inputs(seed: int = 0, part: int = 0) -> dict:
    key_list = jax.random.split(jax.random.key(seed), 6)
    part_splits = jax.random.split(jax.random.fold_in(key_list[5], part), 6)
    latent_tiles = draw_latent_tiles(jax.random.fold_in(jax.random.fold_in(key_list[5], part), 71), part)
    route = draw_route(jax.random.fold_in(jax.random.fold_in(key_list[5], part), 71), part)
    w_query = draw_w_query(jax.random.fold_in(key_list[5], 71), part)
    w_keyval = draw_w_keyval(jax.random.fold_in(key_list[5], 71), part)
    conv_weight = centred(key_list[4], (3, 3, 3, C, C), (27 * C) ** -0.5, 0.0625, ((4, 2),))
    return {"latent_tiles": latent_tiles, "route": route, "w_query": w_query, "w_keyval": w_keyval, "conv_weight": conv_weight}


epsilon = 1e-06

def scaled_rms(values):
    wide = values.astype(jnp.float32)
    return wide / jnp.sqrt(lax.optimization_barrier(jnp.mean(wide * wide, axis=-1, keepdims=True)) + epsilon)

def place_block(tile_block, table):
    inverse = jnp.argsort(table).astype(jnp.int32)
    return jnp.take(tile_block, inverse, axis=0)

def attend_frame(frame_pair):
    query_rows, keyval_rows = frame_pair
    width_c = query_rows.shape[-1]
    scores = jnp.dot(query_rows, keyval_rows[:, :width_c].T, preferred_element_type=jnp.float32) * (1.0 / math.sqrt(width_c))
    largest = lax.optimization_barrier(jnp.max(scores, axis=-1, keepdims=True))
    powers = jnp.exp(scores - largest)
    totals = lax.optimization_barrier(jnp.sum(powers, axis=-1, keepdims=True))
    weights = powers.astype(jnp.bfloat16)
    return jnp.dot(weights, keyval_rows[:, width_c:], preferred_element_type=jnp.float32) / totals

def reference(latent_tiles, route, w_query, w_keyval, conv_weight):
    placed = jax.vmap(place_block)(latent_tiles, route)
    placed = placed.reshape(SPANS, ROWS // RD, FD, RD, W // TCELL, TCELL, C)
    features = placed.transpose(0, 2, 1, 3, 4, 5, 6).reshape(FRAMES, ROWS, W, C)
    normed = scaled_rms(features).astype(jnp.bfloat16)
    flat_cells = normed.reshape(FRAMES * ROWS * W, C)
    queries = jnp.dot(flat_cells, w_query, preferred_element_type=jnp.float32).astype(jnp.bfloat16)
    keyvals = jnp.dot(flat_cells, w_keyval, preferred_element_type=jnp.float32).astype(jnp.bfloat16)
    attended = lax.map(attend_frame, (queries.reshape(FRAMES, ROWS * W, C), keyvals.reshape(FRAMES, ROWS * W, 2 * C)))
    mixed = (features.astype(jnp.float32) + attended.reshape(FRAMES, ROWS, W, C)).astype(jnp.bfloat16)
    activated = jax.nn.silu(scaled_rms(mixed)).astype(jnp.bfloat16)
    padded = jnp.pad(activated.astype(jnp.float32), ((2, 0), (1, 1), (1, 1), (0, 0)))
    conv_sum = lax.conv_general_dilated(padded[None], conv_weight.astype(jnp.float32), (1, 1, 1), 'VALID', dimension_numbers=('NDHWC', 'DHWIO', 'NDHWC'), precision=lax.Precision.HIGHEST)[0]
    return (mixed.astype(jnp.float32) + conv_sum).astype(jnp.bfloat16)
```

```python
import functools
import math

import jax
import jax.numpy as jnp
from jax import lax
from jax.experimental import pallas as pl
from jax.experimental.pallas import tpu as pltpu
from jax.sharding import PartitionSpec as P

C = 384
W = 64
RD = 2
FD = 2
CELLS = FD * RD * W
HALO = FD * (RD + 2) * W
PIECES = 2
KEY_BLOCK = 1024

epsilon = 1e-06
MESH = pl.DeviceIdType.MESH


def scaled_rms(wide):
    return wide / jnp.sqrt(jnp.mean(wide * wide, axis=-1, keepdims=True) + epsilon)


def block_kernel(
    patches,
    spans,
    tiles_ref,
    keys_ref,
    w_query_ref,
    w_keyval_ref,
    conv_ref,
    out_ref,
    tiles,
    keyvals,
    gathered,
    shifted3,
    mixed,
    total,
    w_query,
    w_keyval,
    conv,
    ahead,
    behind,
    load_sem,
    right_send,
    right_recv,
    left_send,
    left_recv,
    pair_send,
    pair_recv,
    span_send,
    span_recv,
):
    z = lax.axis_index("patch")
    x = lax.axis_index("span")
    core = lax.axis_index("chan")
    other = 1 - core
    half = CELLS // 2
    piece = half // PIECES
    band = RD * W

    own_load = pltpu.make_async_copy(tiles_ref, tiles.at[z], load_sem.at[0])
    own_load.start()
    keyval_load = pltpu.make_async_copy(w_keyval_ref, w_keyval, load_sem.at[1])
    keyval_load.start()
    query_load = pltpu.make_async_copy(w_query_ref, w_query, load_sem.at[2])
    query_load.start()
    conv_load = pltpu.make_async_copy(conv_ref, conv, load_sem.at[3])
    conv_load.start()

    barrier = pltpu.get_barrier_semaphore()

    def greet(near, target):
        @pl.when(near)
        def _():
            pl.semaphore_signal(barrier, inc=1, device_id=target, device_id_type=MESH)

    has_left, has_right = z > 0, z < patches - 1
    has_before, has_after = x > 0, x < spans - 1
    greet(has_left, {"patch": z - 1})
    greet(has_right, {"patch": z + 1})
    greet(has_before, {"span": x - 1})
    greet(has_after, {"span": x + 1})
    pl.semaphore_signal(barrier, inc=1, device_id={"chan": other}, device_id_type=MESH)
    near_count = (
        1
        + jnp.where(has_left, 1, 0)
        + jnp.where(has_right, 1, 0)
        + jnp.where(has_before, 1, 0)
        + jnp.where(has_after, 1, 0)
    )
    pl.semaphore_wait(barrier, near_count)

    def part(origin, side, k):
        return tiles.at[origin, pl.ds(pl.multiple_of(side * half + k * piece, piece), piece)]

    def send_right(origin, k):
        return pltpu.make_async_remote_copy(
            part(origin, core, k),
            part(origin, core, k),
            right_send.at[origin, k],
            right_recv.at[origin, k],
            device_id={"patch": z + 1},
            device_id_type=MESH,
        )

    def send_left(origin, k):
        return pltpu.make_async_remote_copy(
            part(origin, core, k),
            part(origin, core, k),
            left_send.at[origin, k],
            left_recv.at[origin, k],
            device_id={"patch": z - 1},
            device_id_type=MESH,
        )

    def send_pair(origin, side, k):
        return pltpu.make_async_remote_copy(
            part(origin, side, k),
            part(origin, side, k),
            pair_send.at[origin, k],
            pair_recv.at[origin, k],
            device_id={"chan": other},
            device_id_type=MESH,
        )

    def when(condition, action):
        @pl.when(condition)
        def _():
            action()

    own_load.wait()
    for k in range(PIECES):
        when(has_right, lambda: send_right(z, k).start())
        when(has_left, lambda: send_left(z, k).start())

    at = lax.broadcasted_iota(jnp.int32, (HALO, 1), 0)
    frame = at // ((RD + 2) * W)
    row = z * RD - 1 + (at // W) % (RD + 2)
    owner = (row + RD) // RD - 1
    wanted = owner * CELLS + (frame * RD + (row + RD) % RD) * W + at % W

    def absorb(origin):
        values = tiles[origin]
        normed = scaled_rms(values.astype(jnp.float32)).astype(jnp.bfloat16)
        keyvals[origin] = jnp.dot(
            normed, w_keyval[...], preferred_element_type=jnp.float32
        ).astype(jnp.bfloat16)
        picks = jnp.where(keys_ref[origin] == wanted, 1.0, 0.0).astype(jnp.bfloat16)
        gathered[...] += jnp.dot(picks, values, preferred_element_type=jnp.float32)

    gathered[...] = jnp.zeros_like(gathered)
    keyval_load.wait()
    absorb(z)

    def absorb_step(step):
        def from_pair(origin):
            for k in range(PIECES):
                send_pair(origin, other, k).wait_recv()
            absorb(origin)

        when(z - step >= 0, lambda: from_pair(z - step))
        when(z + step < patches, lambda: from_pair(z + step))

    def pass_on(step):
        for k in range(PIECES):

            def from_left():
                origin = z - step
                send_right(origin, k).wait_recv()
                when(has_right, lambda: send_right(origin, k).start())
                send_pair(origin, core, k).start()

            def from_right():
                origin = z + step
                send_left(origin, k).wait_recv()
                when(has_left, lambda: send_left(origin, k).start())
                send_pair(origin, core, k).start()

            when(z - step >= 0, from_left)
            when(z + step < patches, from_right)

    pass_on(1)

    def gather_step(step, carry):
        pass_on(step)
        absorb_step(step - 1)
        return carry

    lax.fori_loop(2, patches, gather_step, 0)
    absorb_step(patches - 1)

    query_load.wait()
    queries = jnp.dot(
        scaled_rms(gathered[...]).astype(jnp.bfloat16),
        w_query[...],
        preferred_element_type=jnp.float32,
    ).astype(jnp.bfloat16)
    scale = 1.0 / math.sqrt(C)
    group = min(KEY_BLOCK // CELLS, patches)
    frame_cells = HALO // FD

    def fold(block, carry, f):
        run_max, run_total, run_acc = carry
        first = block * group
        pair = keyvals[pl.ds(first, group)].reshape(group * CELLS, 2 * C)
        codes = keys_ref[pl.ds(first, group)]
        allow = (codes // (RD * W)) % FD == f
        bias = jnp.where(allow, 0.0, -1e30)
        bias = jnp.concatenate([bias[j] for j in range(group)], axis=-1)
        scores = lax.dot_general(
            queries[f * frame_cells : (f + 1) * frame_cells],
            pair[:, :C],
            (((1,), (1,)), ((), ())),
            preferred_element_type=jnp.float32,
        )
        scores = scores * scale + bias
        top = jnp.max(scores, axis=-1, keepdims=True)
        if run_max is not None:
            top = jnp.maximum(top, run_max)
        powers = jnp.exp(scores - top)
        sums = jnp.sum(powers, axis=-1, keepdims=True)
        acc = jnp.dot(
            powers.astype(jnp.bfloat16), pair[:, C:], preferred_element_type=jnp.float32
        )
        if run_max is not None:
            factor = jnp.exp(run_max - top)
            sums = run_total * factor + sums
            acc = run_acc * factor + acc
        return top, sums, acc

    line = lax.broadcasted_iota(jnp.int32, (frame_cells, 1), 0)
    line_row = z * RD - 1 + line // W
    inside = (line_row >= 0) & (line_row < patches * RD)
    for f in range(FD):
        span_of = slice(f * frame_cells, (f + 1) * frame_cells)
        carry = fold(0, (None, None, None), f)
        if patches > group:
            carry = lax.fori_loop(
                1, patches // group, functools.partial(fold, f=f), carry
            )
        _, sums, acc = carry
        rounded = (gathered[span_of] + acc / sums).astype(jnp.bfloat16)
        mixed[span_of] = rounded
        v = scaled_rms(rounded.astype(jnp.float32))
        act = jnp.where(inside, v / (1.0 + jnp.exp(-v)), 0.0)
        before = jnp.where(line % W == 0, 0.0, pltpu.roll(act, 1, 0))
        after = jnp.where(line % W == W - 1, 0.0, pltpu.roll(act, frame_cells - 1, 0))
        shifted3[span_of, 0:C] = before.astype(jnp.bfloat16)
        shifted3[span_of, C : 2 * C] = act.astype(jnp.bfloat16)
        shifted3[span_of, 2 * C : 3 * C] = after.astype(jnp.bfloat16)

    def rows_of(ref, b):
        return jnp.concatenate(
            [ref[f * frame_cells + b * W : f * frame_cells + b * W + band] for f in range(FD)],
            axis=0,
        )

    def conv_time(a):
        result = None
        for b in range(3):
            term = jnp.dot(
                rows_of(shifted3, b), conv[3 * a + b], preferred_element_type=jnp.float32
            )
            result = term if result is None else result + term
        return result

    def send_span(t):
        return pltpu.make_async_remote_copy(
            ahead.at[t],
            behind.at[t],
            span_send.at[t],
            span_recv.at[t],
            device_id={"span": x + 1},
            device_id_type=MESH,
        )

    conv_load.wait()
    oldest = conv_time(0)
    ahead[1] = oldest[band:].astype(jnp.bfloat16)
    when(has_after, lambda: send_span(1).start())
    middle = conv_time(1)
    ahead[0] = (oldest[:band] + middle[band:]).astype(jnp.bfloat16)
    when(has_after, lambda: send_span(0).start())
    width = out_ref.shape[-1]
    pick_from = lax.broadcasted_iota(jnp.int32, (C, width), 0)
    pick_to = lax.broadcasted_iota(jnp.int32, (C, width), 1) + core * width
    picks = jnp.where(pick_from == pick_to, 1.0, 0.0).astype(jnp.bfloat16)
    newest = conv_time(2) + jnp.dot(
        rows_of(mixed, 1), picks, preferred_element_type=jnp.float32
    )
    total[0:band] = newest[:band]
    total[band : 2 * band] = newest[band:] + middle[:band]

    @pl.when(x == 0)
    def _():
        out_ref[...] = total[...].astype(jnp.bfloat16)

    @pl.when(has_before)
    def _():
        for t in range(FD):
            send_span(t).wait_recv()
            here = slice(t * band, (t + 1) * band)
            out_ref[here] = (total[here] + behind[t].astype(jnp.float32)).astype(jnp.bfloat16)

    @pl.when(has_after)
    def _():
        for t in range(FD):
            send_span(t).wait_send()

    def finish(step, carry):
        for k in range(PIECES):

            def left_origin():
                when(has_right, lambda: send_right(z - step, k).wait_send())
                when(step > 0, lambda: send_pair(z - step, core, k).wait_send())

            def right_origin():
                when(has_left, lambda: send_left(z + step, k).wait_send())
                when(step > 0, lambda: send_pair(z + step, core, k).wait_send())

            when(z - step >= 0, left_origin)
            when(z + step < patches, right_origin)
        return carry

    lax.fori_loop(0, patches, finish, 0)


def local(latent_tiles, route, w_query, w_keyval, conv_weight):
    patches = lax.axis_size("patch")
    spans = lax.axis_size("span")
    width = conv_weight.shape[-1]
    tiles_own = latent_tiles.reshape(CELLS, C)
    tile_cells = latent_tiles.shape[2]
    keys = (
        route.reshape(patches, -1, 1) * tile_cells + jnp.arange(tile_cells, dtype=jnp.int32)
    ).reshape(patches, 1, CELLS)
    bf16, f32 = jnp.bfloat16, jnp.float32
    dma = pltpu.SemaphoreType.DMA
    anywhere = pl.BlockSpec(memory_space=pl.ANY)
    vmem = pl.BlockSpec(memory_space=pltpu.VMEM)
    result = pl.pallas_call(
        functools.partial(block_kernel, patches, spans),
        out_shape=jax.ShapeDtypeStruct((FD * RD * W, width), bf16),
        in_specs=[anywhere, vmem, anywhere, anywhere, anywhere],
        out_specs=vmem,
        scratch_shapes=[
            pltpu.VMEM((patches, CELLS, C), bf16),
            pltpu.VMEM((patches, CELLS, 2 * C), bf16),
            pltpu.VMEM((HALO, C), f32),
            pltpu.VMEM((HALO, 3 * C), bf16),
            pltpu.VMEM((HALO, C), bf16),
            pltpu.VMEM((FD * RD * W, width), f32),
            pltpu.VMEM((C, C), bf16),
            pltpu.VMEM((C, 2 * C), bf16),
            pltpu.VMEM((9, 3 * C, width), bf16),
            pltpu.VMEM((FD, RD * W, width), bf16),
            pltpu.VMEM((FD, RD * W, width), bf16),
            dma((4,)),
            dma((patches, PIECES)),
            dma((patches, PIECES)),
            dma((patches, PIECES)),
            dma((patches, PIECES)),
            dma((patches, PIECES)),
            dma((patches, PIECES)),
            dma((FD,)),
            dma((FD,)),
        ],
        compiler_params=pltpu.CompilerParams(
            collective_id=0, has_side_effects=True, vmem_limit_bytes=56 * 1024 * 1024
        ),
    )(tiles_own, keys, w_query, w_keyval, conv_weight.reshape(9, 3 * C, width))
    return result.reshape(FD, RD, W, width)


def solution(mesh):
    placed = (
        P(("clips", "span"), "patch", None, None),
        P(("clips", "span"), None),
        P(),
        P(),
        P(None, None, None, None, "chan"),
    )
    return jax.shard_map(
        local,
        mesh=mesh,
        in_specs=placed,
        out_specs=P(("clips", "span"), "patch", None, "chan"),
        check_vma=False,
    )
```

```python
import functools
import math

import jax
import jax.numpy as jnp
from jax import lax
from jax.experimental import pallas as pl
from jax.experimental.pallas import tpu as pltpu
from jax.sharding import PartitionSpec as P

C = 384
W = 64
RD = 2
FD = 2
CELLS = FD * RD * W
HALO = FD * (RD + 2) * W
PIECES = 2
KEY_BLOCK = 1024

epsilon = 1e-06
MESH = pl.DeviceIdType.MESH


def scaled_rms(wide):
    return wide / jnp.sqrt(jnp.mean(wide * wide, axis=-1, keepdims=True) + epsilon)


def block_kernel(
    patches,
    spans,
    tiles_ref,
    route_ref,
    w_query_ref,
    w_keyval_ref,
    conv_ref,
    out_ref,
    raw,
    places_of,
    keys_ref,
    tiles,
    keyvals,
    gathered,
    shifted3,
    mixed,
    total,
    w_query,
    w_keyval,
    conv,
    ahead,
    behind,
    load_sem,
    right_send,
    right_recv,
    left_send,
    left_recv,
    pair_send,
    pair_recv,
    span_send,
    span_recv,
):
    z = lax.axis_index("patch")
    x = lax.axis_index("span")
    core = lax.axis_index("chan")
    other = 1 - core
    half = CELLS // 2
    piece = half // PIECES
    band = RD * W

    own_load = pltpu.make_async_copy(tiles_ref, raw, load_sem.at[0])
    own_load.start()
    keyval_load = pltpu.make_async_copy(w_keyval_ref, w_keyval, load_sem.at[1])
    keyval_load.start()
    route_load = pltpu.make_async_copy(route_ref, places_of, load_sem.at[4])
    route_load.start()
    query_load = pltpu.make_async_copy(w_query_ref, w_query, load_sem.at[2])
    query_load.start()
    conv_load = pltpu.make_async_copy(conv_ref, conv, load_sem.at[3])
    conv_load.start()

    barrier = pltpu.get_barrier_semaphore()
    here, tile_cells = raw.shape[0], raw.shape[1]

    def greet(near, target):
        @pl.when(near)
        def _():
            pl.semaphore_signal(barrier, inc=1, device_id=target, device_id_type=MESH)

    has_left, has_right = z > 0, z < patches - 1
    has_before, has_after = x > 0, x < spans - 1
    greet(has_left, {"patch": z - 1})
    greet(has_right, {"patch": z + 1})
    greet(has_before, {"span": x - 1})
    greet(has_after, {"span": x + 1})
    pl.semaphore_signal(barrier, inc=1, device_id={"chan": other}, device_id_type=MESH)
    near_count = (
        1
        + jnp.where(has_left, 1, 0)
        + jnp.where(has_right, 1, 0)
        + jnp.where(has_before, 1, 0)
        + jnp.where(has_after, 1, 0)
    )
    pl.semaphore_wait(barrier, near_count)

    def part(origin, side, k):
        return tiles.at[origin, pl.ds(pl.multiple_of(side * half + k * piece, piece), piece)]

    def send_right(origin, k):
        return pltpu.make_async_remote_copy(
            part(origin, core, k),
            part(origin, core, k),
            right_send.at[origin, k],
            right_recv.at[origin, k],
            device_id={"patch": z + 1},
            device_id_type=MESH,
        )

    def send_left(origin, k):
        return pltpu.make_async_remote_copy(
            part(origin, core, k),
            part(origin, core, k),
            left_send.at[origin, k],
            left_recv.at[origin, k],
            device_id={"patch": z - 1},
            device_id_type=MESH,
        )

    def send_pair(origin, side, k):
        return pltpu.make_async_remote_copy(
            part(origin, side, k),
            part(origin, side, k),
            pair_send.at[origin, k],
            pair_recv.at[origin, k],
            device_id={"chan": other},
            device_id_type=MESH,
        )

    def when(condition, action):
        @pl.when(condition)
        def _():
            action()

    own_load.wait()
    tiles[z] = raw[...].reshape(CELLS, C)
    for k in range(PIECES):
        when(has_right, lambda: send_right(z, k).start())
        when(has_left, lambda: send_left(z, k).start())

    at = lax.broadcasted_iota(jnp.int32, (HALO, 1), 0)
    frame = at // ((RD + 2) * W)
    row = z * RD - 1 + (at // W) % (RD + 2)
    owner = (row + RD) // RD - 1
    wanted = owner * CELLS + (frame * RD + (row + RD) % RD) * W + at % W

    def absorb(origin):
        values = tiles[origin]
        normed = scaled_rms(values.astype(jnp.float32)).astype(jnp.bfloat16)
        keyvals[origin] = jnp.dot(
            normed, w_keyval[...], preferred_element_type=jnp.float32
        ).astype(jnp.bfloat16)
        picks = jnp.where(keys_ref[origin] == wanted, 1.0, 0.0).astype(jnp.bfloat16)
        gathered[...] += jnp.dot(picks, values, preferred_element_type=jnp.float32)

    lanes = 2 * here
    spread_from = lax.broadcasted_iota(jnp.int32, (lanes, 2 * CELLS), 0)
    spread_to = lax.broadcasted_iota(jnp.int32, (lanes, 2 * CELLS), 1)
    spread = jnp.where(spread_to // tile_cells == spread_from, 1.0, 0.0).astype(jnp.bfloat16)
    cell = lax.broadcasted_iota(jnp.int32, (1, 2 * CELLS), 1) % tile_cells
    route_load.wait()
    for j in range(patches // 2):
        places = places_of[:, j * lanes : (j + 1) * lanes]
        digits = jnp.concatenate(
            [jnp.broadcast_to(d, (8, lanes)) for d in (places // 256, places % 256)], axis=0
        )
        wide = jnp.dot(
            digits.astype(jnp.float32).astype(jnp.bfloat16),
            spread,
            preferred_element_type=jnp.float32,
        )
        place = (wide[0:1] * 256.0 + wide[8:9]).astype(jnp.int32)
        codes = place * tile_cells + cell
        keys_ref[2 * j] = codes[:, :CELLS]
        keys_ref[2 * j + 1] = codes[:, CELLS:]

    gathered[...] = jnp.zeros_like(gathered)
    keyval_load.wait()
    absorb(z)

    def absorb_step(step):
        def from_pair(origin):
            for k in range(PIECES):
                send_pair(origin, other, k).wait_recv()
            absorb(origin)

        when(z - step >= 0, lambda: from_pair(z - step))
        when(z + step < patches, lambda: from_pair(z + step))

    def pass_on(step):
        for k in range(PIECES):

            def from_left():
                origin = z - step
                send_right(origin, k).wait_recv()
                when(has_right, lambda: send_right(origin, k).start())
                send_pair(origin, core, k).start()

            def from_right():
                origin = z + step
                send_left(origin, k).wait_recv()
                when(has_left, lambda: send_left(origin, k).start())
                send_pair(origin, core, k).start()

            when(z - step >= 0, from_left)
            when(z + step < patches, from_right)

    pass_on(1)

    def gather_step(step, carry):
        pass_on(step)
        absorb_step(step - 1)
        return carry

    lax.fori_loop(2, patches, gather_step, 0)
    absorb_step(patches - 1)

    query_load.wait()
    queries = jnp.dot(
        scaled_rms(gathered[...]).astype(jnp.bfloat16),
        w_query[...],
        preferred_element_type=jnp.float32,
    ).astype(jnp.bfloat16)
    scale = 1.0 / math.sqrt(C)
    group = min(KEY_BLOCK // CELLS, patches)
    frame_cells = HALO // FD

    def fold(block, carry, f):
        run_max, run_total, run_acc = carry
        first = block * group
        pair = keyvals[pl.ds(first, group)].reshape(group * CELLS, 2 * C)
        codes = keys_ref[pl.ds(first, group)]
        allow = (codes // (RD * W)) % FD == f
        bias = jnp.where(allow, 0.0, -1e30)
        bias = jnp.concatenate([bias[j] for j in range(group)], axis=-1)
        scores = lax.dot_general(
            queries[f * frame_cells : (f + 1) * frame_cells],
            pair[:, :C],
            (((1,), (1,)), ((), ())),
            preferred_element_type=jnp.float32,
        )
        scores = scores * scale + bias
        top = jnp.max(scores, axis=-1, keepdims=True)
        if run_max is not None:
            top = jnp.maximum(top, run_max)
        powers = jnp.exp(scores - top)
        sums = jnp.sum(powers, axis=-1, keepdims=True)
        acc = jnp.dot(
            powers.astype(jnp.bfloat16), pair[:, C:], preferred_element_type=jnp.float32
        )
        if run_max is not None:
            factor = jnp.exp(run_max - top)
            sums = run_total * factor + sums
            acc = run_acc * factor + acc
        return top, sums, acc

    line = lax.broadcasted_iota(jnp.int32, (frame_cells, 1), 0)
    line_row = z * RD - 1 + line // W
    inside = (line_row >= 0) & (line_row < patches * RD)
    for f in range(FD):
        span_of = slice(f * frame_cells, (f + 1) * frame_cells)
        carry = fold(0, (None, None, None), f)
        if patches > group:
            carry = lax.fori_loop(
                1, patches // group, functools.partial(fold, f=f), carry
            )
        _, sums, acc = carry
        rounded = (gathered[span_of] + acc / sums).astype(jnp.bfloat16)
        mixed[span_of] = rounded
        v = scaled_rms(rounded.astype(jnp.float32))
        act = jnp.where(inside, v / (1.0 + jnp.exp(-v)), 0.0)
        before = jnp.where(line % W == 0, 0.0, pltpu.roll(act, 1, 0))
        after = jnp.where(line % W == W - 1, 0.0, pltpu.roll(act, frame_cells - 1, 0))
        shifted3[span_of, 0:C] = before.astype(jnp.bfloat16)
        shifted3[span_of, C : 2 * C] = act.astype(jnp.bfloat16)
        shifted3[span_of, 2 * C : 3 * C] = after.astype(jnp.bfloat16)

    def rows_of(ref, b):
        return jnp.concatenate(
            [ref[f * frame_cells + b * W : f * frame_cells + b * W + band] for f in range(FD)],
            axis=0,
        )

    def conv_time(a):
        result = None
        for b in range(3):
            at_tap = 3 * (3 * a + b)
            weights = jnp.concatenate([conv[at_tap + c] for c in range(3)], axis=-1)
            term = lax.dot_general(
                rows_of(shifted3, b),
                weights,
                (((1,), (1,)), ((), ())),
                preferred_element_type=jnp.float32,
            )
            result = term if result is None else result + term
        return result

    def send_span(t):
        return pltpu.make_async_remote_copy(
            ahead.at[t],
            behind.at[t],
            span_send.at[t],
            span_recv.at[t],
            device_id={"span": x + 1},
            device_id_type=MESH,
        )

    conv_load.wait()
    oldest = conv_time(0)
    ahead[1] = oldest[band:].astype(jnp.bfloat16)
    when(has_after, lambda: send_span(1).start())
    middle = conv_time(1)
    ahead[0] = (oldest[:band] + middle[band:]).astype(jnp.bfloat16)
    when(has_after, lambda: send_span(0).start())
    width = out_ref.shape[-1]
    pick_from = lax.broadcasted_iota(jnp.int32, (C, width), 0)
    pick_to = lax.broadcasted_iota(jnp.int32, (C, width), 1) + core * width
    picks = jnp.where(pick_from == pick_to, 1.0, 0.0).astype(jnp.bfloat16)
    newest = conv_time(2) + jnp.dot(
        rows_of(mixed, 1), picks, preferred_element_type=jnp.float32
    )
    total[0:band] = newest[:band]
    total[band : 2 * band] = newest[band:] + middle[:band]

    @pl.when(x == 0)
    def _():
        out_ref[...] = total[...].astype(jnp.bfloat16)

    @pl.when(has_before)
    def _():
        for t in range(FD):
            send_span(t).wait_recv()
            here = slice(t * band, (t + 1) * band)
            out_ref[here] = (total[here] + behind[t].astype(jnp.float32)).astype(jnp.bfloat16)

    @pl.when(has_after)
    def _():
        for t in range(FD):
            send_span(t).wait_send()

    def finish(step, carry):
        for k in range(PIECES):

            def left_origin():
                when(has_right, lambda: send_right(z - step, k).wait_send())
                when(step > 0, lambda: send_pair(z - step, core, k).wait_send())

            def right_origin():
                when(has_left, lambda: send_left(z + step, k).wait_send())
                when(step > 0, lambda: send_pair(z + step, core, k).wait_send())

            when(z - step >= 0, left_origin)
            when(z + step < patches, right_origin)
        return carry

    lax.fori_loop(0, patches, finish, 0)


def local(latent_tiles, route, w_query, w_keyval, conv_weight):
    patches = lax.axis_size("patch")
    spans = lax.axis_size("span")
    width = conv_weight.shape[-1]
    tiles_here, tile_cells = latent_tiles.shape[1:3]
    bf16, f32 = jnp.bfloat16, jnp.float32
    dma = pltpu.SemaphoreType.DMA
    anywhere = pl.BlockSpec(memory_space=pl.ANY)
    vmem = pl.BlockSpec(memory_space=pltpu.VMEM)
    result = pl.pallas_call(
        functools.partial(block_kernel, patches, spans),
        out_shape=pltpu.VMEM((FD * RD * W, width), bf16),
        in_specs=[anywhere] * 5,
        out_specs=vmem,
        scratch_shapes=[
            pltpu.VMEM((tiles_here, tile_cells, C), bf16),
            pltpu.VMEM(route.shape, jnp.int32),
            pltpu.VMEM((patches, 1, CELLS), jnp.int32),
            pltpu.VMEM((patches, CELLS, C), bf16),
            pltpu.VMEM((patches, CELLS, 2 * C), bf16),
            pltpu.VMEM((HALO, C), f32),
            pltpu.VMEM((HALO, 3 * C), bf16),
            pltpu.VMEM((HALO, C), bf16),
            pltpu.VMEM((FD * RD * W, width), f32),
            pltpu.VMEM((C, C), bf16),
            pltpu.VMEM((C, 2 * C), bf16),
            pltpu.VMEM((27, width, C), bf16),
            pltpu.VMEM((FD, RD * W, width), bf16),
            pltpu.VMEM((FD, RD * W, width), bf16),
            dma((5,)),
            dma((patches, PIECES)),
            dma((patches, PIECES)),
            dma((patches, PIECES)),
            dma((patches, PIECES)),
            dma((patches, PIECES)),
            dma((patches, PIECES)),
            dma((FD,)),
            dma((FD,)),
        ],
        compiler_params=pltpu.CompilerParams(
            collective_id=0, has_side_effects=True, vmem_limit_bytes=56 * 1024 * 1024
        ),
    )(
        latent_tiles.reshape(tiles_here, tile_cells, C),
        route,
        w_query,
        w_keyval,
        conv_weight.transpose(0, 1, 2, 4, 3).reshape(27, width, C),
    )
    return result.reshape(FD, RD, W, width)


def solution(mesh):
    placed = (
        P(("clips", "span"), "patch", None, None),
        P(("clips", "span"), None),
        P(),
        P(),
        P(None, None, None, None, "chan"),
    )
    return jax.shard_map(
        local,
        mesh=mesh,
        in_specs=placed,
        out_specs=P(("clips", "span"), "patch", None, "chan"),
        check_vma=False,
    )
```

```python
import functools
import math

import jax
import jax.numpy as jnp
from jax import lax
from jax.experimental import pallas as pl
from jax.experimental.pallas import tpu as pltpu
from jax.sharding import PartitionSpec as P

C = 384
W = 64
RD = 2
FD = 2
CELLS = FD * RD * W
HALO = FD * (RD + 2) * W
PIECES = 2
KEY_BLOCK = 1024

epsilon = 1e-06
MESH = pl.DeviceIdType.MESH


def scaled_rms(wide):
    return wide / jnp.sqrt(jnp.mean(wide * wide, axis=-1, keepdims=True) + epsilon)


def block_kernel(
    patches,
    spans,
    tiles_ref,
    route_ref,
    w_query_ref,
    w_keyval_ref,
    conv_ref,
    out_ref,
    places_of,
    keys_ref,
    tiles,
    keyvals,
    gathered,
    shifted3,
    mixed,
    total,
    w_query,
    w_keyval,
    conv,
    ahead,
    behind,
    load_sem,
    right_send,
    right_recv,
    left_send,
    left_recv,
    pair_send,
    pair_recv,
    span_send,
    span_recv,
):
    z = lax.axis_index("patch")
    x = lax.axis_index("span")
    core = lax.axis_index("chan")
    other = 1 - core
    half = tiles.shape[1] // 2
    piece = half // PIECES
    band = RD * W

    barrier = pltpu.get_barrier_semaphore()
    here, tile_cells = tiles.shape[1], tiles.shape[2]

    def greet(near, target):
        @pl.when(near)
        def _():
            pl.semaphore_signal(barrier, inc=1, device_id=target, device_id_type=MESH)

    has_left, has_right = z > 0, z < patches - 1
    has_before, has_after = x > 0, x < spans - 1
    greet(has_left, {"patch": z - 1})
    greet(has_right, {"patch": z + 1})
    greet(has_before, {"span": x - 1})
    greet(has_after, {"span": x + 1})
    pl.semaphore_signal(barrier, inc=1, device_id={"chan": other}, device_id_type=MESH)

    own_load = pltpu.make_async_copy(tiles_ref, tiles.at[z], load_sem.at[0])
    own_load.start()
    keyval_load = pltpu.make_async_copy(w_keyval_ref, w_keyval, load_sem.at[1])
    keyval_load.start()
    route_load = pltpu.make_async_copy(route_ref, places_of, load_sem.at[4])
    route_load.start()
    query_load = pltpu.make_async_copy(w_query_ref, w_query, load_sem.at[2])
    query_load.start()
    conv_load = pltpu.make_async_copy(conv_ref, conv, load_sem.at[3])
    conv_load.start()

    near_count = (
        1
        + jnp.where(has_left, 1, 0)
        + jnp.where(has_right, 1, 0)
        + jnp.where(has_before, 1, 0)
        + jnp.where(has_after, 1, 0)
    )
    pl.semaphore_wait(barrier, near_count)

    def part(origin, side, k):
        return tiles.at[origin, pl.ds(side * half + k * piece, piece)]

    def own_part(k):
        return tiles_ref.at[pl.ds(core * half + k * piece, piece)]

    def send_right(origin, k, own=False):
        return pltpu.make_async_remote_copy(
            own_part(k) if own else part(origin, core, k),
            part(origin, core, k),
            right_send.at[origin, k],
            right_recv.at[origin, k],
            device_id={"patch": z + 1},
            device_id_type=MESH,
        )

    def send_left(origin, k, own=False):
        return pltpu.make_async_remote_copy(
            own_part(k) if own else part(origin, core, k),
            part(origin, core, k),
            left_send.at[origin, k],
            left_recv.at[origin, k],
            device_id={"patch": z - 1},
            device_id_type=MESH,
        )

    def send_pair(origin, side, k):
        return pltpu.make_async_remote_copy(
            part(origin, side, k),
            part(origin, side, k),
            pair_send.at[origin, k],
            pair_recv.at[origin, k],
            device_id={"chan": other},
            device_id_type=MESH,
        )

    def when(condition, action):
        @pl.when(condition)
        def _():
            action()

    for k in range(PIECES):
        when(has_right, lambda: send_right(z, k, own=True).start())
        when(has_left, lambda: send_left(z, k, own=True).start())

    at = lax.broadcasted_iota(jnp.int32, (HALO, 1), 0)
    frame = at // ((RD + 2) * W)
    row = z * RD - 1 + (at // W) % (RD + 2)
    owner = (row + RD) // RD - 1
    wanted = owner * CELLS + (frame * RD + (row + RD) % RD) * W + at % W

    def absorb(origin):
        values = tiles[origin].reshape(CELLS, C)
        normed = scaled_rms(values.astype(jnp.float32)).astype(jnp.bfloat16)
        keyvals[origin] = jnp.dot(
            normed, w_keyval[...], preferred_element_type=jnp.float32
        ).astype(jnp.bfloat16)
        picks = jnp.where(keys_ref[origin] == wanted, 1.0, 0.0).astype(jnp.bfloat16)
        gathered[...] += jnp.dot(picks, values, preferred_element_type=jnp.float32)

    lanes = 2 * here
    spread_from = lax.broadcasted_iota(jnp.int32, (lanes, 2 * CELLS), 0)
    spread_to = lax.broadcasted_iota(jnp.int32, (lanes, 2 * CELLS), 1)
    spread = jnp.where(spread_to // tile_cells == spread_from, 1.0, 0.0).astype(jnp.bfloat16)
    cell = lax.broadcasted_iota(jnp.int32, (1, 2 * CELLS), 1) % tile_cells
    route_load.wait()
    for j in range(patches // 2):
        places = places_of[:, j * lanes : (j + 1) * lanes]
        digits = jnp.concatenate(
            [jnp.broadcast_to(d, (8, lanes)) for d in (places // 256, places % 256)], axis=0
        )
        wide = jnp.dot(
            digits.astype(jnp.float32).astype(jnp.bfloat16),
            spread,
            preferred_element_type=jnp.float32,
        )
        place = (wide[0:1] * 256.0 + wide[8:9]).astype(jnp.int32)
        codes = place * tile_cells + cell
        keys_ref[2 * j] = codes[:, :CELLS]
        keys_ref[2 * j + 1] = codes[:, CELLS:]

    gathered[...] = jnp.zeros_like(gathered)
    keyval_load.wait()
    own_load.wait()
    absorb(z)

    def absorb_step(step):
        def from_pair(origin):
            for k in range(PIECES):
                send_pair(origin, other, k).wait_recv()
            absorb(origin)

        when(z - step >= 0, lambda: from_pair(z - step))
        when(z + step < patches, lambda: from_pair(z + step))

    def pass_on(step):
        for k in range(PIECES):

            def from_left():
                origin = z - step
                send_right(origin, k).wait_recv()
                when(has_right, lambda: send_right(origin, k).start())
                send_pair(origin, core, k).start()

            def from_right():
                origin = z + step
                send_left(origin, k).wait_recv()
                when(has_left, lambda: send_left(origin, k).start())
                send_pair(origin, core, k).start()

            when(z - step >= 0, from_left)
            when(z + step < patches, from_right)

    pass_on(1)

    def gather_step(step, carry):
        pass_on(step)
        absorb_step(step - 1)
        return carry

    lax.fori_loop(2, patches, gather_step, 0)
    absorb_step(patches - 1)

    query_load.wait()
    queries = jnp.dot(
        scaled_rms(gathered[...]).astype(jnp.bfloat16),
        w_query[...],
        preferred_element_type=jnp.float32,
    ).astype(jnp.bfloat16)
    scale = 1.0 / math.sqrt(C)
    group = min(KEY_BLOCK // CELLS, patches)
    frame_cells = HALO // FD

    def fold(block, carry, f):
        run_max, run_total, run_acc = carry
        first = block * group
        pair = keyvals[pl.ds(first, group)].reshape(group * CELLS, 2 * C)
        codes = keys_ref[pl.ds(first, group)]
        allow = (codes // (RD * W)) % FD == f
        bias = jnp.where(allow, 0.0, -1e30)
        bias = jnp.concatenate([bias[j] for j in range(group)], axis=-1)
        scores = lax.dot_general(
            queries[f * frame_cells : (f + 1) * frame_cells],
            pair[:, :C],
            (((1,), (1,)), ((), ())),
            preferred_element_type=jnp.float32,
        )
        scores = scores * scale + bias
        top = jnp.max(scores, axis=-1, keepdims=True)
        if run_max is not None:
            top = jnp.maximum(top, run_max)
        powers = jnp.exp(scores - top)
        sums = jnp.sum(powers, axis=-1, keepdims=True)
        acc = jnp.dot(
            powers.astype(jnp.bfloat16), pair[:, C:], preferred_element_type=jnp.float32
        )
        if run_max is not None:
            factor = jnp.exp(run_max - top)
            sums = run_total * factor + sums
            acc = run_acc * factor + acc
        return top, sums, acc

    line = lax.broadcasted_iota(jnp.int32, (frame_cells, 1), 0)
    line_row = z * RD - 1 + line // W
    inside = (line_row >= 0) & (line_row < patches * RD)
    for f in range(FD):
        span_of = slice(f * frame_cells, (f + 1) * frame_cells)
        carry = fold(0, (None, None, None), f)
        if patches > group:
            carry = lax.fori_loop(
                1, patches // group, functools.partial(fold, f=f), carry
            )
        _, sums, acc = carry
        rounded = (gathered[span_of] + acc / sums).astype(jnp.bfloat16)
        mixed[span_of] = rounded
        v = scaled_rms(rounded.astype(jnp.float32))
        act = jnp.where(inside, v / (1.0 + jnp.exp(-v)), 0.0)
        before = jnp.where(line % W == 0, 0.0, pltpu.roll(act, 1, 0))
        after = jnp.where(line % W == W - 1, 0.0, pltpu.roll(act, frame_cells - 1, 0))
        shifted3[span_of, 0:C] = before.astype(jnp.bfloat16)
        shifted3[span_of, C : 2 * C] = act.astype(jnp.bfloat16)
        shifted3[span_of, 2 * C : 3 * C] = after.astype(jnp.bfloat16)

    def rows_of(ref, b):
        return jnp.concatenate(
            [ref[f * frame_cells + b * W : f * frame_cells + b * W + band] for f in range(FD)],
            axis=0,
        )

    def conv_time(a):
        result = None
        for b in range(3):
            at_tap = 3 * (3 * a + b)
            weights = jnp.concatenate([conv[at_tap + c] for c in range(3)], axis=-1)
            term = lax.dot_general(
                rows_of(shifted3, b),
                weights,
                (((1,), (1,)), ((), ())),
                preferred_element_type=jnp.float32,
            )
            result = term if result is None else result + term
        return result

    def send_span(t):
        return pltpu.make_async_remote_copy(
            ahead.at[t],
            behind.at[t],
            span_send.at[t],
            span_recv.at[t],
            device_id={"span": x + 1},
            device_id_type=MESH,
        )

    conv_load.wait()
    oldest = conv_time(0)
    ahead[1] = oldest[band:].astype(jnp.bfloat16)
    when(has_after, lambda: send_span(1).start())
    middle = conv_time(1)
    ahead[0] = (oldest[:band] + middle[band:]).astype(jnp.bfloat16)
    when(has_after, lambda: send_span(0).start())
    width = out_ref.shape[-1]
    pick_from = lax.broadcasted_iota(jnp.int32, (C, width), 0)
    pick_to = lax.broadcasted_iota(jnp.int32, (C, width), 1) + core * width
    picks = jnp.where(pick_from == pick_to, 1.0, 0.0).astype(jnp.bfloat16)
    newest = conv_time(2) + jnp.dot(
        rows_of(mixed, 1), picks, preferred_element_type=jnp.float32
    )
    total[0:band] = newest[:band]
    total[band : 2 * band] = newest[band:] + middle[:band]

    @pl.when(x == 0)
    def _():
        out_ref[...] = total[...].astype(jnp.bfloat16)

    @pl.when(has_before)
    def _():
        for t in range(FD):
            send_span(t).wait_recv()
            here = slice(t * band, (t + 1) * band)
            out_ref[here] = (total[here] + behind[t].astype(jnp.float32)).astype(jnp.bfloat16)

    @pl.when(has_after)
    def _():
        for t in range(FD):
            send_span(t).wait_send()

    def finish(step, carry):
        for k in range(PIECES):

            def left_origin():
                when(has_right, lambda: send_right(z - step, k).wait_send())
                when(step > 0, lambda: send_pair(z - step, core, k).wait_send())

            def right_origin():
                when(has_left, lambda: send_left(z + step, k).wait_send())
                when(step > 0, lambda: send_pair(z + step, core, k).wait_send())

            when(z - step >= 0, left_origin)
            when(z + step < patches, right_origin)
        return carry

    lax.fori_loop(0, patches, finish, 0)


def local(latent_tiles, route, w_query, w_keyval, conv_weight):
    patches = lax.axis_size("patch")
    spans = lax.axis_size("span")
    width = conv_weight.shape[-1]
    tiles_here, tile_cells = latent_tiles.shape[1:3]
    bf16, f32 = jnp.bfloat16, jnp.float32
    dma = pltpu.SemaphoreType.DMA
    anywhere = pl.BlockSpec(memory_space=pl.ANY)
    vmem = pl.BlockSpec(memory_space=pltpu.VMEM)
    result = pl.pallas_call(
        functools.partial(block_kernel, patches, spans),
        out_shape=pltpu.VMEM((FD * RD * W, width), bf16),
        in_specs=[anywhere] * 5,
        out_specs=vmem,
        scratch_shapes=[
            pltpu.VMEM(route.shape, jnp.int32),
            pltpu.VMEM((patches, 1, CELLS), jnp.int32),
            pltpu.VMEM((patches, tiles_here, tile_cells, C), bf16),
            pltpu.VMEM((patches, CELLS, 2 * C), bf16),
            pltpu.VMEM((HALO, C), f32),
            pltpu.VMEM((HALO, 3 * C), bf16),
            pltpu.VMEM((HALO, C), bf16),
            pltpu.VMEM((FD * RD * W, width), f32),
            pltpu.VMEM((C, C), bf16),
            pltpu.VMEM((C, 2 * C), bf16),
            pltpu.VMEM((27, width, C), bf16),
            pltpu.VMEM((FD, RD * W, width), bf16),
            pltpu.VMEM((FD, RD * W, width), bf16),
            dma((5,)),
            dma((patches, PIECES)),
            dma((patches, PIECES)),
            dma((patches, PIECES)),
            dma((patches, PIECES)),
            dma((patches, PIECES)),
            dma((patches, PIECES)),
            dma((FD,)),
            dma((FD,)),
        ],
        compiler_params=pltpu.CompilerParams(
            collective_id=0, has_side_effects=True, vmem_limit_bytes=56 * 1024 * 1024
        ),
    )(
        latent_tiles.reshape(tiles_here, tile_cells, C),
        route,
        w_query,
        w_keyval,
        conv_weight.transpose(0, 1, 2, 4, 3).reshape(27, width, C),
    )
    return result.reshape(FD, RD, W, width)


def solution(mesh):
    placed = (
        P(("clips", "span"), "patch", None, None),
        P(("clips", "span"), None),
        P(),
        P(),
        P(None, None, None, None, "chan"),
    )
    return jax.shard_map(
        local,
        mesh=mesh,
        in_specs=placed,
        out_specs=P(("clips", "span"), "patch", None, "chan"),
        check_vma=False,
    )
```

```python
import functools
import math

import jax
import jax.numpy as jnp
from jax import lax
from jax.experimental import pallas as pl
from jax.experimental.pallas import tpu as pltpu
from jax.sharding import PartitionSpec as P

C = 384
W = 64
RD = 2
FD = 2
CELLS = FD * RD * W
HALO = FD * (RD + 2) * W
SHARE = HALO // 2
PIECES = 2
KEY_BLOCK = 1024

epsilon = 1e-06
MESH = pl.DeviceIdType.MESH


def scaled_rms(wide):
    return wide / jnp.sqrt(jnp.mean(wide * wide, axis=-1, keepdims=True) + epsilon)


def block_kernel(
    patches,
    spans,
    tiles_ref,
    route_ref,
    w_query_ref,
    w_keyval_ref,
    conv_ref,
    out_ref,
    places_of,
    keys_ref,
    tiles,
    keyvals,
    gathered,
    shifted3,
    mixed,
    total,
    w_query,
    w_keyval,
    conv,
    ahead,
    behind,
    load_sem,
    right_send,
    right_recv,
    left_send,
    left_recv,
    pair_send,
    pair_recv,
    span_send,
    span_recv,
    mixed_send,
    mixed_recv,
):
    z = lax.axis_index("patch")
    x = lax.axis_index("span")
    core = lax.axis_index("chan")
    other = 1 - core
    half = tiles.shape[1] // 2
    piece = half // PIECES
    band = RD * W

    barrier = pltpu.get_barrier_semaphore()
    here, tile_cells = tiles.shape[1], tiles.shape[2]

    def greet(near, target):
        @pl.when(near)
        def _():
            pl.semaphore_signal(barrier, inc=1, device_id=target, device_id_type=MESH)

    has_left, has_right = z > 0, z < patches - 1
    has_before, has_after = x > 0, x < spans - 1
    greet(has_left, {"patch": z - 1})
    greet(has_right, {"patch": z + 1})
    greet(has_before, {"span": x - 1})
    greet(has_after, {"span": x + 1})
    pl.semaphore_signal(barrier, inc=1, device_id={"chan": other}, device_id_type=MESH)

    own_load = pltpu.make_async_copy(tiles_ref, tiles.at[z], load_sem.at[0])
    own_load.start()
    keyval_load = pltpu.make_async_copy(w_keyval_ref, w_keyval, load_sem.at[1])
    keyval_load.start()
    route_load = pltpu.make_async_copy(route_ref, places_of, load_sem.at[4])
    route_load.start()
    query_load = pltpu.make_async_copy(w_query_ref, w_query, load_sem.at[2])
    query_load.start()
    conv_load = pltpu.make_async_copy(conv_ref, conv, load_sem.at[3])
    conv_load.start()

    near_count = (
        1
        + jnp.where(has_left, 1, 0)
        + jnp.where(has_right, 1, 0)
        + jnp.where(has_before, 1, 0)
        + jnp.where(has_after, 1, 0)
    )
    pl.semaphore_wait(barrier, near_count)

    def part(origin, side, k):
        return tiles.at[origin, pl.ds(side * half + k * piece, piece)]

    def own_part(k):
        return tiles_ref.at[pl.ds(core * half + k * piece, piece)]

    def send_right(origin, k, own=False):
        return pltpu.make_async_remote_copy(
            own_part(k) if own else part(origin, core, k),
            part(origin, core, k),
            right_send.at[origin, k],
            right_recv.at[origin, k],
            device_id={"patch": z + 1},
            device_id_type=MESH,
        )

    def send_left(origin, k, own=False):
        return pltpu.make_async_remote_copy(
            own_part(k) if own else part(origin, core, k),
            part(origin, core, k),
            left_send.at[origin, k],
            left_recv.at[origin, k],
            device_id={"patch": z - 1},
            device_id_type=MESH,
        )

    def send_pair(origin, side, k):
        return pltpu.make_async_remote_copy(
            part(origin, side, k),
            part(origin, side, k),
            pair_send.at[origin, k],
            pair_recv.at[origin, k],
            device_id={"chan": other},
            device_id_type=MESH,
        )

    def when(condition, action):
        @pl.when(condition)
        def _():
            action()

    for k in range(PIECES):
        when(has_right, lambda: send_right(z, k, own=True).start())
        when(has_left, lambda: send_left(z, k, own=True).start())

    rows_share = (RD + 2) // 2
    at = lax.broadcasted_iota(jnp.int32, (SHARE, 1), 0)
    frame = at // (rows_share * W)
    row = z * RD - 1 + core * rows_share + (at // W) % rows_share
    owner = (row + RD) // RD - 1
    wanted = owner * CELLS + (frame * RD + (row + RD) % RD) * W + at % W

    def absorb(origin):
        values = tiles[origin].reshape(CELLS, C)
        normed = scaled_rms(values.astype(jnp.float32)).astype(jnp.bfloat16)
        keyvals[origin] = jnp.dot(
            normed, w_keyval[...], preferred_element_type=jnp.float32
        ).astype(jnp.bfloat16)
        picks = jnp.where(keys_ref[origin] == wanted, 1.0, 0.0).astype(jnp.bfloat16)
        gathered[...] += jnp.dot(picks, values, preferred_element_type=jnp.float32)

    lanes = 2 * here
    spread_from = lax.broadcasted_iota(jnp.int32, (lanes, 2 * CELLS), 0)
    spread_to = lax.broadcasted_iota(jnp.int32, (lanes, 2 * CELLS), 1)
    spread = jnp.where(spread_to // tile_cells == spread_from, 1.0, 0.0).astype(jnp.bfloat16)
    cell = lax.broadcasted_iota(jnp.int32, (1, 2 * CELLS), 1) % tile_cells
    route_load.wait()
    for j in range(patches // 2):
        places = places_of[:, j * lanes : (j + 1) * lanes]
        digits = jnp.concatenate(
            [jnp.broadcast_to(d, (8, lanes)) for d in (places // 256, places % 256)], axis=0
        )
        wide = jnp.dot(
            digits.astype(jnp.float32).astype(jnp.bfloat16),
            spread,
            preferred_element_type=jnp.float32,
        )
        place = (wide[0:1] * 256.0 + wide[8:9]).astype(jnp.int32)
        codes = place * tile_cells + cell
        keys_ref[2 * j] = codes[:, :CELLS]
        keys_ref[2 * j + 1] = codes[:, CELLS:]

    gathered[...] = jnp.zeros_like(gathered)
    keyval_load.wait()
    own_load.wait()
    absorb(z)

    def absorb_step(step):
        def from_pair(origin):
            for k in range(PIECES):
                send_pair(origin, other, k).wait_recv()
            absorb(origin)

        when(z - step >= 0, lambda: from_pair(z - step))
        when(z + step < patches, lambda: from_pair(z + step))

    def pass_on(step):
        for k in range(PIECES):

            def from_left():
                origin = z - step
                send_right(origin, k).wait_recv()
                when(has_right, lambda: send_right(origin, k).start())
                send_pair(origin, core, k).start()

            def from_right():
                origin = z + step
                send_left(origin, k).wait_recv()
                when(has_left, lambda: send_left(origin, k).start())
                send_pair(origin, core, k).start()

            when(z - step >= 0, from_left)
            when(z + step < patches, from_right)

    pass_on(1)

    def gather_step(step, carry):
        pass_on(step)
        absorb_step(step - 1)
        return carry

    lax.fori_loop(2, patches, gather_step, 0)
    absorb_step(patches - 1)

    query_load.wait()
    queries = jnp.dot(
        scaled_rms(gathered[...]).astype(jnp.bfloat16),
        w_query[...],
        preferred_element_type=jnp.float32,
    ).astype(jnp.bfloat16)
    scale = 1.0 / math.sqrt(C)
    group = min(KEY_BLOCK // CELLS, patches)
    frame_cells = HALO // FD
    share_cells = SHARE // FD

    def fold(block, carry, f):
        run_max, run_total, run_acc = carry
        first = block * group
        pair = keyvals[pl.ds(first, group)].reshape(group * CELLS, 2 * C)
        codes = keys_ref[pl.ds(first, group)]
        allow = (codes // (RD * W)) % FD == f
        bias = jnp.where(allow, 0.0, -1e30)
        bias = jnp.concatenate([bias[j] for j in range(group)], axis=-1)
        scores = lax.dot_general(
            queries[f * share_cells : (f + 1) * share_cells],
            pair[:, :C],
            (((1,), (1,)), ((), ())),
            preferred_element_type=jnp.float32,
        )
        scores = scores * scale + bias
        top = jnp.max(scores, axis=-1, keepdims=True)
        if run_max is not None:
            top = jnp.maximum(top, run_max)
        powers = jnp.exp(scores - top)
        sums = jnp.sum(powers, axis=-1, keepdims=True)
        acc = jnp.dot(
            powers.astype(jnp.bfloat16), pair[:, C:], preferred_element_type=jnp.float32
        )
        if run_max is not None:
            factor = jnp.exp(run_max - top)
            sums = run_total * factor + sums
            acc = run_acc * factor + acc
        return top, sums, acc

    line = lax.broadcasted_iota(jnp.int32, (share_cells, 1), 0)

    def share_at(f, side):
        return pl.ds(pl.multiple_of(f * frame_cells + side * share_cells, share_cells), share_cells)

    def send_mixed(f, side):
        return pltpu.make_async_remote_copy(
            mixed.at[share_at(f, side)],
            mixed.at[share_at(f, side)],
            mixed_send.at[f],
            mixed_recv.at[f],
            device_id={"chan": other},
            device_id_type=MESH,
        )

    def attend(f):
        carry = fold(0, (None, None, None), f)
        if patches > group:
            carry = lax.fori_loop(
                1, patches // group, functools.partial(fold, f=f), carry
            )
        _, sums, acc = carry
        features = gathered[f * share_cells : (f + 1) * share_cells]
        mixed[share_at(f, core)] = (features + acc / sums).astype(jnp.bfloat16)
        send_mixed(f, core).start()

    def activate(f, side):
        here = share_at(f, side)
        line_row = z * RD - 1 + side * rows_share + line // W
        inside = (line_row >= 0) & (line_row < patches * RD)
        v = scaled_rms(mixed[here].astype(jnp.float32))
        act = jnp.where(inside, v / (1.0 + jnp.exp(-v)), 0.0)
        before = jnp.where(line % W == 0, 0.0, pltpu.roll(act, 1, 0))
        after = jnp.where(line % W == W - 1, 0.0, pltpu.roll(act, share_cells - 1, 0))
        shifted3[here, 0:C] = before.astype(jnp.bfloat16)
        shifted3[here, C : 2 * C] = act.astype(jnp.bfloat16)
        shifted3[here, 2 * C : 3 * C] = after.astype(jnp.bfloat16)

    def conv_time(f, a):
        result = None
        for b in range(3):
            at_tap = 3 * (3 * a + b)
            weights = jnp.concatenate([conv[at_tap + c] for c in range(3)], axis=-1)
            first = f * frame_cells + b * W
            term = lax.dot_general(
                shifted3[first : first + band],
                weights,
                (((1,), (1,)), ((), ())),
                preferred_element_type=jnp.float32,
            )
            result = term if result is None else result + term
        return result

    def send_span(t):
        return pltpu.make_async_remote_copy(
            ahead.at[t],
            behind.at[t],
            span_send.at[t],
            span_recv.at[t],
            device_id={"span": x + 1},
            device_id_type=MESH,
        )

    width = out_ref.shape[-1]
    pick_from = lax.broadcasted_iota(jnp.int32, (C, width), 0)
    pick_to = lax.broadcasted_iota(jnp.int32, (C, width), 1) + core * width
    picks = jnp.where(pick_from == pick_to, 1.0, 0.0).astype(jnp.bfloat16)

    def own_mixed(f):
        first = f * frame_cells + W
        return jnp.dot(
            mixed[first : first + band], picks, preferred_element_type=jnp.float32
        )

    attend(1)
    activate(1, core)
    attend(0)
    activate(0, core)
    conv_load.wait()
    send_mixed(1, other).wait_recv()
    activate(1, other)
    ahead[1] = conv_time(1, 0).astype(jnp.bfloat16)
    when(has_after, lambda: send_span(1).start())
    middle = conv_time(1, 1)
    send_mixed(0, other).wait_recv()
    activate(0, other)
    ahead[0] = (conv_time(0, 0) + middle).astype(jnp.bfloat16)
    when(has_after, lambda: send_span(0).start())
    total[0:band] = conv_time(0, 2) + own_mixed(0)
    total[band : 2 * band] = conv_time(0, 1) + conv_time(1, 2) + own_mixed(1)

    @pl.when(x == 0)
    def _():
        out_ref[...] = total[...].astype(jnp.bfloat16)

    @pl.when(has_before)
    def _():
        for t in range(FD):
            send_span(t).wait_recv()
            here = slice(t * band, (t + 1) * band)
            out_ref[here] = (total[here] + behind[t].astype(jnp.float32)).astype(jnp.bfloat16)

    @pl.when(has_after)
    def _():
        for t in range(FD):
            send_span(t).wait_send()

    def finish(step, carry):
        for k in range(PIECES):

            def left_origin():
                when(has_right, lambda: send_right(z - step, k).wait_send())
                when(step > 0, lambda: send_pair(z - step, core, k).wait_send())

            def right_origin():
                when(has_left, lambda: send_left(z + step, k).wait_send())
                when(step > 0, lambda: send_pair(z + step, core, k).wait_send())

            when(z - step >= 0, left_origin)
            when(z + step < patches, right_origin)
        return carry

    lax.fori_loop(0, patches, finish, 0)
    for f in range(FD):
        send_mixed(f, core).wait_send()


def local(latent_tiles, route, w_query, w_keyval, conv_weight):
    patches = lax.axis_size("patch")
    spans = lax.axis_size("span")
    width = conv_weight.shape[-1]
    tiles_here, tile_cells = latent_tiles.shape[1:3]
    bf16, f32 = jnp.bfloat16, jnp.float32
    dma = pltpu.SemaphoreType.DMA
    anywhere = pl.BlockSpec(memory_space=pl.ANY)
    vmem = pl.BlockSpec(memory_space=pltpu.VMEM)
    result = pl.pallas_call(
        functools.partial(block_kernel, patches, spans),
        out_shape=pltpu.VMEM((FD * RD * W, width), bf16),
        in_specs=[anywhere] * 5,
        out_specs=vmem,
        scratch_shapes=[
            pltpu.VMEM(route.shape, jnp.int32),
            pltpu.VMEM((patches, 1, CELLS), jnp.int32),
            pltpu.VMEM((patches, tiles_here, tile_cells, C), bf16),
            pltpu.VMEM((patches, CELLS, 2 * C), bf16),
            pltpu.VMEM((SHARE, C), f32),
            pltpu.VMEM((HALO, 3 * C), bf16),
            pltpu.VMEM((HALO, C), bf16),
            pltpu.VMEM((FD * RD * W, width), f32),
            pltpu.VMEM((C, C), bf16),
            pltpu.VMEM((C, 2 * C), bf16),
            pltpu.VMEM((27, width, C), bf16),
            pltpu.VMEM((FD, RD * W, width), bf16),
            pltpu.VMEM((FD, RD * W, width), bf16),
            dma((5,)),
            dma((patches, PIECES)),
            dma((patches, PIECES)),
            dma((patches, PIECES)),
            dma((patches, PIECES)),
            dma((patches, PIECES)),
            dma((patches, PIECES)),
            dma((FD,)),
            dma((FD,)),
            dma((FD,)),
            dma((FD,)),
        ],
        compiler_params=pltpu.CompilerParams(
            collective_id=0, has_side_effects=True, vmem_limit_bytes=56 * 1024 * 1024
        ),
    )(
        latent_tiles.reshape(tiles_here, tile_cells, C),
        route,
        w_query,
        w_keyval,
        conv_weight.transpose(0, 1, 2, 4, 3).reshape(27, width, C),
    )
    return result.reshape(FD, RD, W, width)


def solution(mesh):
    placed = (
        P(("clips", "span"), "patch", None, None),
        P(("clips", "span"), None),
        P(),
        P(),
        P(None, None, None, None, "chan"),
    )
    return jax.shard_map(
        local,
        mesh=mesh,
        in_specs=placed,
        out_specs=P(("clips", "span"), "patch", None, "chan"),
        check_vma=False,
    )
```

```python
import functools
import math

import jax
import jax.numpy as jnp
from jax import lax
from jax.experimental import pallas as pl
from jax.experimental.pallas import tpu as pltpu
from jax.sharding import PartitionSpec as P

C = 384
W = 64
RD = 2
FD = 2
CELLS = FD * RD * W
HALO = FD * (RD + 2) * W
SHARE = HALO // 2
PIECES = 2
KEY_BLOCK = 1024

epsilon = 1e-06
MESH = pl.DeviceIdType.MESH


def scaled_rms(wide):
    return wide * (1.0 / jnp.sqrt(jnp.mean(wide * wide, axis=-1, keepdims=True) + epsilon))


def block_kernel(
    patches,
    spans,
    tiles_ref,
    route_ref,
    w_query_ref,
    w_keyval_ref,
    conv_ref,
    out_ref,
    raw,
    places_of,
    keys_ref,
    tiles,
    keyvals,
    gathered,
    shifted3,
    mixed,
    total,
    w_query,
    w_keyval,
    conv,
    ahead,
    behind,
    load_sem,
    right_send,
    right_recv,
    left_send,
    left_recv,
    pair_send,
    pair_recv,
    span_send,
    span_recv,
    mixed_send,
    mixed_recv,
):
    z = lax.axis_index("patch")
    x = lax.axis_index("span")
    core = lax.axis_index("chan")
    other = 1 - core
    half = CELLS // 2
    piece = half // PIECES
    band = RD * W

    barrier = pltpu.get_barrier_semaphore()
    here, tile_cells = raw.shape[0], raw.shape[1]

    def greet(near, target):
        @pl.when(near)
        def _():
            pl.semaphore_signal(barrier, inc=1, device_id=target, device_id_type=MESH)

    has_left, has_right = z > 0, z < patches - 1
    has_before, has_after = x > 0, x < spans - 1
    greet(has_left, {"patch": z - 1})
    greet(has_right, {"patch": z + 1})
    greet(has_before, {"span": x - 1})
    greet(has_after, {"span": x + 1})
    pl.semaphore_signal(barrier, inc=1, device_id={"chan": other}, device_id_type=MESH)

    own_load = pltpu.make_async_copy(tiles_ref, raw, load_sem.at[0])
    own_load.start()
    keyval_load = pltpu.make_async_copy(w_keyval_ref, w_keyval, load_sem.at[1])
    keyval_load.start()
    route_load = pltpu.make_async_copy(route_ref, places_of, load_sem.at[4])
    route_load.start()
    query_load = pltpu.make_async_copy(w_query_ref, w_query, load_sem.at[2])
    query_load.start()
    conv_load = pltpu.make_async_copy(conv_ref, conv, load_sem.at[3])
    conv_load.start()

    near_count = (
        1
        + jnp.where(has_left, 1, 0)
        + jnp.where(has_right, 1, 0)
        + jnp.where(has_before, 1, 0)
        + jnp.where(has_after, 1, 0)
    )
    own_load.wait()
    tiles[z] = raw[...].reshape(CELLS, C)
    pl.semaphore_wait(barrier, near_count)

    def part(origin, side, k):
        return tiles.at[origin, pl.ds(pl.multiple_of(side * half + k * piece, piece), piece)]

    def send_right(origin, k):
        return pltpu.make_async_remote_copy(
            part(origin, core, k),
            part(origin, core, k),
            right_send.at[origin, k],
            right_recv.at[origin, k],
            device_id={"patch": z + 1},
            device_id_type=MESH,
        )

    def send_left(origin, k):
        return pltpu.make_async_remote_copy(
            part(origin, core, k),
            part(origin, core, k),
            left_send.at[origin, k],
            left_recv.at[origin, k],
            device_id={"patch": z - 1},
            device_id_type=MESH,
        )

    def send_pair(origin, side, k):
        return pltpu.make_async_remote_copy(
            part(origin, side, k),
            part(origin, side, k),
            pair_send.at[origin, k],
            pair_recv.at[origin, k],
            device_id={"chan": other},
            device_id_type=MESH,
        )

    def when(condition, action):
        @pl.when(condition)
        def _():
            action()

    for k in range(PIECES):
        when(has_right, lambda: send_right(z, k).start())
        when(has_left, lambda: send_left(z, k).start())

    rows_share = (RD + 2) // 2
    at = lax.broadcasted_iota(jnp.int32, (SHARE, 1), 0)
    frame = at // (rows_share * W)
    row = z * RD - 1 + core * rows_share + (at // W) % rows_share
    owner = (row + RD) // RD - 1
    wanted = owner * CELLS + (frame * RD + (row + RD) % RD) * W + at % W

    def absorb(origin):
        values = tiles[origin]
        normed = scaled_rms(values.astype(jnp.float32)).astype(jnp.bfloat16)
        keyvals[origin] = jnp.dot(
            normed, w_keyval[...], preferred_element_type=jnp.float32
        ).astype(jnp.bfloat16)
        picks = jnp.where(keys_ref[origin] == wanted, 1.0, 0.0).astype(jnp.bfloat16)
        gathered[...] += jnp.dot(picks, values, preferred_element_type=jnp.float32)

    lanes = 2 * here
    spread_from = lax.broadcasted_iota(jnp.int32, (lanes, 2 * CELLS), 0)
    spread_to = lax.broadcasted_iota(jnp.int32, (lanes, 2 * CELLS), 1)
    spread = jnp.where(spread_to // tile_cells == spread_from, 1.0, 0.0).astype(jnp.bfloat16)
    cell = lax.broadcasted_iota(jnp.int32, (1, 2 * CELLS), 1) % tile_cells
    route_load.wait()
    for j in range(patches // 2):
        places = places_of[:, j * lanes : (j + 1) * lanes]
        digits = jnp.concatenate(
            [jnp.broadcast_to(d, (8, lanes)) for d in (places // 256, places % 256)], axis=0
        )
        wide = jnp.dot(
            digits.astype(jnp.float32).astype(jnp.bfloat16),
            spread,
            preferred_element_type=jnp.float32,
        )
        place = (wide[0:1] * 256.0 + wide[8:9]).astype(jnp.int32)
        codes = place * tile_cells + cell
        keys_ref[2 * j] = codes[:, :CELLS]
        keys_ref[2 * j + 1] = codes[:, CELLS:]

    gathered[...] = jnp.zeros_like(gathered)
    keyval_load.wait()
    absorb(z)

    def absorb_step(step):
        def from_pair(origin):
            for k in range(PIECES):
                send_pair(origin, other, k).wait_recv()
            absorb(origin)

        when(z - step >= 0, lambda: from_pair(z - step))
        when(z + step < patches, lambda: from_pair(z + step))

    def pass_on(step):
        for k in range(PIECES):

            def from_left():
                origin = z - step
                send_right(origin, k).wait_recv()
                when(has_right, lambda: send_right(origin, k).start())
                send_pair(origin, core, k).start()

            def from_right():
                origin = z + step
                send_left(origin, k).wait_recv()
                when(has_left, lambda: send_left(origin, k).start())
                send_pair(origin, core, k).start()

            when(z - step >= 0, from_left)
            when(z + step < patches, from_right)

    pass_on(1)
    inner = has_left & has_right

    def gather_step(step, carry):
        when(jnp.logical_not(inner), lambda: absorb_step(step - 1))
        pass_on(step)
        when(inner, lambda: absorb_step(step - 1))
        return carry

    lax.fori_loop(2, patches, gather_step, 0)
    absorb_step(patches - 1)

    query_load.wait()
    queries = jnp.dot(
        scaled_rms(gathered[...]).astype(jnp.bfloat16),
        w_query[...],
        preferred_element_type=jnp.float32,
    ).astype(jnp.bfloat16)
    scale = 1.0 / math.sqrt(C)
    group = min(KEY_BLOCK // CELLS, patches)
    frame_cells = HALO // FD
    share_cells = SHARE // FD

    def fold(block, carry, f):
        run_max, run_total, run_acc = carry
        first = block * group
        pair = keyvals[pl.ds(first, group)].reshape(group * CELLS, 2 * C)
        codes = keys_ref[pl.ds(first, group)]
        allow = (codes // (RD * W)) % FD == f
        bias = jnp.where(allow, 0.0, -1e30)
        bias = jnp.concatenate([bias[j] for j in range(group)], axis=-1)
        scores = lax.dot_general(
            queries[f * share_cells : (f + 1) * share_cells],
            pair[:, :C],
            (((1,), (1,)), ((), ())),
            preferred_element_type=jnp.float32,
        )
        scores = scores * scale + bias
        top = jnp.max(scores, axis=-1, keepdims=True)
        if run_max is not None:
            top = jnp.maximum(top, run_max)
        powers = jnp.exp(scores - top)
        sums = jnp.sum(powers, axis=-1, keepdims=True)
        acc = jnp.dot(
            powers.astype(jnp.bfloat16), pair[:, C:], preferred_element_type=jnp.float32
        )
        if run_max is not None:
            factor = jnp.exp(run_max - top)
            sums = run_total * factor + sums
            acc = run_acc * factor + acc
        return top, sums, acc

    line = lax.broadcasted_iota(jnp.int32, (share_cells, 1), 0)

    def share_at(f, side):
        return pl.ds(pl.multiple_of(f * frame_cells + side * share_cells, share_cells), share_cells)

    def send_mixed(f, side):
        return pltpu.make_async_remote_copy(
            mixed.at[share_at(f, side)],
            mixed.at[share_at(f, side)],
            mixed_send.at[f],
            mixed_recv.at[f],
            device_id={"chan": other},
            device_id_type=MESH,
        )

    def attend(f):
        carry = fold(0, (None, None, None), f)
        if patches > group:
            carry = lax.fori_loop(
                1, patches // group, functools.partial(fold, f=f), carry
            )
        _, sums, acc = carry
        features = gathered[f * share_cells : (f + 1) * share_cells]
        mixed[share_at(f, core)] = (features + acc * (1.0 / sums)).astype(jnp.bfloat16)
        send_mixed(f, core).start()

    def activate(f, side):
        here = share_at(f, side)
        line_row = z * RD - 1 + side * rows_share + line // W
        inside = (line_row >= 0) & (line_row < patches * RD)
        v = scaled_rms(mixed[here].astype(jnp.float32))
        act = jnp.where(inside, (0.5 * v) * (1.0 + jnp.tanh(0.5 * v)), 0.0)
        before = jnp.where(line % W == 0, 0.0, pltpu.roll(act, 1, 0))
        after = jnp.where(line % W == W - 1, 0.0, pltpu.roll(act, share_cells - 1, 0))
        shifted3[here, 0:C] = before.astype(jnp.bfloat16)
        shifted3[here, C : 2 * C] = act.astype(jnp.bfloat16)
        shifted3[here, 2 * C : 3 * C] = after.astype(jnp.bfloat16)

    def conv_time(f, a):
        result = None
        for b in range(3):
            at_tap = 3 * (3 * a + b)
            weights = jnp.concatenate([conv[at_tap + c] for c in range(3)], axis=-1)
            first = f * frame_cells + b * W
            term = lax.dot_general(
                shifted3[first : first + band],
                weights,
                (((1,), (1,)), ((), ())),
                preferred_element_type=jnp.float32,
            )
            result = term if result is None else result + term
        return result

    def send_span(t):
        return pltpu.make_async_remote_copy(
            ahead.at[t],
            behind.at[t],
            span_send.at[t],
            span_recv.at[t],
            device_id={"span": x + 1},
            device_id_type=MESH,
        )

    width = out_ref.shape[-1]
    pick_from = lax.broadcasted_iota(jnp.int32, (C, width), 0)
    pick_to = lax.broadcasted_iota(jnp.int32, (C, width), 1) + core * width
    picks = jnp.where(pick_from == pick_to, 1.0, 0.0).astype(jnp.bfloat16)

    def own_mixed(f):
        first = f * frame_cells + W
        return jnp.dot(
            mixed[first : first + band], picks, preferred_element_type=jnp.float32
        )

    attend(1)
    activate(1, core)
    attend(0)
    activate(0, core)
    conv_load.wait()
    send_mixed(1, other).wait_recv()
    activate(1, other)
    ahead[1] = conv_time(1, 0).astype(jnp.bfloat16)
    when(has_after, lambda: send_span(1).start())
    middle = conv_time(1, 1)
    send_mixed(0, other).wait_recv()
    activate(0, other)
    ahead[0] = (conv_time(0, 0) + middle).astype(jnp.bfloat16)
    when(has_after, lambda: send_span(0).start())
    total[0:band] = conv_time(0, 2) + own_mixed(0)
    total[band : 2 * band] = conv_time(0, 1) + conv_time(1, 2) + own_mixed(1)

    @pl.when(x == 0)
    def _():
        out_ref[...] = total[...].astype(jnp.bfloat16)

    @pl.when(has_before)
    def _():
        for t in range(FD):
            send_span(t).wait_recv()
            here = slice(t * band, (t + 1) * band)
            out_ref[here] = (total[here] + behind[t].astype(jnp.float32)).astype(jnp.bfloat16)

    @pl.when(has_after)
    def _():
        for t in range(FD):
            send_span(t).wait_send()

    def finish(step, carry):
        for k in range(PIECES):

            def left_origin():
                when(has_right, lambda: send_right(z - step, k).wait_send())
                when(step > 0, lambda: send_pair(z - step, core, k).wait_send())

            def right_origin():
                when(has_left, lambda: send_left(z + step, k).wait_send())
                when(step > 0, lambda: send_pair(z + step, core, k).wait_send())

            when(z - step >= 0, left_origin)
            when(z + step < patches, right_origin)
        return carry

    lax.fori_loop(0, patches, finish, 0)
    for f in range(FD):
        send_mixed(f, core).wait_send()


def local(latent_tiles, route, w_query, w_keyval, conv_weight):
    patches = lax.axis_size("patch")
    spans = lax.axis_size("span")
    width = conv_weight.shape[-1]
    tiles_here, tile_cells = latent_tiles.shape[1:3]
    bf16, f32 = jnp.bfloat16, jnp.float32
    dma = pltpu.SemaphoreType.DMA
    anywhere = pl.BlockSpec(memory_space=pl.ANY)
    vmem = pl.BlockSpec(memory_space=pltpu.VMEM)
    result = pl.pallas_call(
        functools.partial(block_kernel, patches, spans),
        out_shape=pltpu.VMEM((FD * RD * W, width), bf16),
        in_specs=[anywhere] * 5,
        out_specs=vmem,
        scratch_shapes=[
            pltpu.VMEM((tiles_here, tile_cells, C), bf16),
            pltpu.VMEM(route.shape, jnp.int32),
            pltpu.VMEM((patches, 1, CELLS), jnp.int32),
            pltpu.VMEM((patches, CELLS, C), bf16),
            pltpu.VMEM((patches, CELLS, 2 * C), bf16),
            pltpu.VMEM((SHARE, C), f32),
            pltpu.VMEM((HALO, 3 * C), bf16),
            pltpu.VMEM((HALO, C), bf16),
            pltpu.VMEM((FD * RD * W, width), f32),
            pltpu.VMEM((C, C), bf16),
            pltpu.VMEM((C, 2 * C), bf16),
            pltpu.VMEM((27, width, C), bf16),
            pltpu.VMEM((FD, RD * W, width), bf16),
            pltpu.VMEM((FD, RD * W, width), bf16),
            dma((5,)),
            dma((patches, PIECES)),
            dma((patches, PIECES)),
            dma((patches, PIECES)),
            dma((patches, PIECES)),
            dma((patches, PIECES)),
            dma((patches, PIECES)),
            dma((FD,)),
            dma((FD,)),
            dma((FD,)),
            dma((FD,)),
        ],
        compiler_params=pltpu.CompilerParams(
            collective_id=0, has_side_effects=True, vmem_limit_bytes=56 * 1024 * 1024
        ),
    )(
        latent_tiles.reshape(tiles_here, tile_cells, C),
        route,
        w_query,
        w_keyval,
        conv_weight.transpose(0, 1, 2, 4, 3).reshape(27, width, C),
    )
    return result.reshape(FD, RD, W, width)


def solution(mesh):
    placed = (
        P(("clips", "span"), "patch", None, None),
        P(("clips", "span"), None),
        P(),
        P(),
        P(None, None, None, None, "chan"),
    )
    return jax.shard_map(
        local,
        mesh=mesh,
        in_specs=placed,
        out_specs=P(("clips", "span"), "patch", None, "chan"),
        check_vma=False,
    )
```

```python
import functools
import math

import jax
import jax.numpy as jnp
from jax import lax
from jax.experimental import pallas as pl
from jax.experimental.pallas import tpu as pltpu
from jax.sharding import PartitionSpec as P

C = 384
W = 64
RD = 2
FD = 2
CELLS = FD * RD * W
HALO = FD * (RD + 2) * W
SHARE = HALO // 2
PIECES = 4
KEY_BLOCK = 1024

epsilon = 1e-06
MESH = pl.DeviceIdType.MESH


def scaled_rms(wide):
    return wide * (1.0 / jnp.sqrt(jnp.mean(wide * wide, axis=-1, keepdims=True) + epsilon))


def block_kernel(
    patches,
    spans,
    tiles_ref,
    route_ref,
    w_query_ref,
    w_keyval_ref,
    conv_ref,
    out_ref,
    raw,
    places_of,
    keys_ref,
    tiles,
    keyvals,
    gathered,
    shifted3,
    mixed,
    total,
    w_query,
    w_keyval,
    conv,
    ahead,
    behind,
    load_sem,
    right_send,
    right_recv,
    left_send,
    left_recv,
    pair_send,
    pair_recv,
    span_send,
    span_recv,
    mixed_send,
    mixed_recv,
):
    z = lax.axis_index("patch")
    x = lax.axis_index("span")
    core = lax.axis_index("chan")
    other = 1 - core
    half = CELLS // 2
    piece = half // PIECES
    band = RD * W

    barrier = pltpu.get_barrier_semaphore()
    here, tile_cells = raw.shape[0], raw.shape[1]

    def greet(near, target):
        @pl.when(near)
        def _():
            pl.semaphore_signal(barrier, inc=1, device_id=target, device_id_type=MESH)

    has_left, has_right = z > 0, z < patches - 1
    has_before, has_after = x > 0, x < spans - 1
    greet(has_left, {"patch": z - 1})
    greet(has_right, {"patch": z + 1})
    greet(has_before, {"span": x - 1})
    greet(has_after, {"span": x + 1})
    pl.semaphore_signal(barrier, inc=1, device_id={"chan": other}, device_id_type=MESH)

    own_load = pltpu.make_async_copy(tiles_ref, raw, load_sem.at[0])
    own_load.start()
    keyval_load = pltpu.make_async_copy(w_keyval_ref, w_keyval, load_sem.at[1])
    keyval_load.start()
    route_load = pltpu.make_async_copy(route_ref, places_of, load_sem.at[4])
    route_load.start()
    query_load = pltpu.make_async_copy(w_query_ref, w_query, load_sem.at[2])
    query_load.start()
    conv_load = pltpu.make_async_copy(conv_ref, conv, load_sem.at[3])
    conv_load.start()

    near_count = (
        1
        + jnp.where(has_left, 1, 0)
        + jnp.where(has_right, 1, 0)
        + jnp.where(has_before, 1, 0)
        + jnp.where(has_after, 1, 0)
    )
    own_load.wait()
    tiles[z] = raw[...].reshape(CELLS, C)
    pl.semaphore_wait(barrier, near_count)

    def part(origin, side, k):
        return tiles.at[origin, pl.ds(pl.multiple_of(side * half + k * piece, piece), piece)]

    def send_right(origin, k):
        return pltpu.make_async_remote_copy(
            part(origin, core, k),
            part(origin, core, k),
            right_send.at[origin, k],
            right_recv.at[origin, k],
            device_id={"patch": z + 1},
            device_id_type=MESH,
        )

    def send_left(origin, k):
        return pltpu.make_async_remote_copy(
            part(origin, core, k),
            part(origin, core, k),
            left_send.at[origin, k],
            left_recv.at[origin, k],
            device_id={"patch": z - 1},
            device_id_type=MESH,
        )

    def send_pair(origin, side, k):
        return pltpu.make_async_remote_copy(
            part(origin, side, k),
            part(origin, side, k),
            pair_send.at[origin, k],
            pair_recv.at[origin, k],
            device_id={"chan": other},
            device_id_type=MESH,
        )

    def when(condition, action):
        @pl.when(condition)
        def _():
            action()

    for k in range(PIECES):
        when(has_right, lambda: send_right(z, k).start())
        when(has_left, lambda: send_left(z, k).start())

    rows_share = (RD + 2) // 2
    at = lax.broadcasted_iota(jnp.int32, (SHARE, 1), 0)
    frame = at // (rows_share * W)
    row = z * RD - 1 + core * rows_share + (at // W) % rows_share
    owner = (row + RD) // RD - 1
    wanted = owner * CELLS + (frame * RD + (row + RD) % RD) * W + at % W

    def absorb(origin):
        values = tiles[origin]
        normed = scaled_rms(values.astype(jnp.float32)).astype(jnp.bfloat16)
        keyvals[origin] = jnp.dot(
            normed, w_keyval[...], preferred_element_type=jnp.float32
        ).astype(jnp.bfloat16)
        picks = jnp.where(keys_ref[origin] == wanted, 1.0, 0.0).astype(jnp.bfloat16)
        gathered[...] += jnp.dot(picks, values, preferred_element_type=jnp.float32)

    lanes = 2 * here
    spread_from = lax.broadcasted_iota(jnp.int32, (lanes, 2 * CELLS), 0)
    spread_to = lax.broadcasted_iota(jnp.int32, (lanes, 2 * CELLS), 1)
    spread = jnp.where(spread_to // tile_cells == spread_from, 1.0, 0.0).astype(jnp.bfloat16)
    cell = lax.broadcasted_iota(jnp.int32, (1, 2 * CELLS), 1) % tile_cells
    route_load.wait()
    for j in range(patches // 2):
        places = places_of[:, j * lanes : (j + 1) * lanes]
        digits = jnp.concatenate(
            [jnp.broadcast_to(d, (8, lanes)) for d in (places // 256, places % 256)], axis=0
        )
        wide = jnp.dot(
            digits.astype(jnp.float32).astype(jnp.bfloat16),
            spread,
            preferred_element_type=jnp.float32,
        )
        place = (wide[0:1] * 256.0 + wide[8:9]).astype(jnp.int32)
        codes = place * tile_cells + cell
        keys_ref[2 * j] = codes[:, :CELLS]
        keys_ref[2 * j + 1] = codes[:, CELLS:]

    gathered[...] = jnp.zeros_like(gathered)
    keyval_load.wait()
    absorb(z)

    def absorb_step(step):
        def from_pair(origin):
            for k in range(PIECES):
                send_pair(origin, other, k).wait_recv()
            absorb(origin)

        when(z - step >= 0, lambda: from_pair(z - step))
        when(z + step < patches, lambda: from_pair(z + step))

    def pass_on(step):
        for k in range(PIECES):

            def from_left():
                origin = z - step
                send_right(origin, k).wait_recv()
                when(has_right, lambda: send_right(origin, k).start())
                send_pair(origin, core, k).start()

            def from_right():
                origin = z + step
                send_left(origin, k).wait_recv()
                when(has_left, lambda: send_left(origin, k).start())
                send_pair(origin, core, k).start()

            when(z - step >= 0, from_left)
            when(z + step < patches, from_right)

    pass_on(1)
    inner = has_left & has_right

    def gather_step(step, carry):
        when(jnp.logical_not(inner), lambda: absorb_step(step - 1))
        pass_on(step)
        when(inner, lambda: absorb_step(step - 1))
        return carry

    lax.fori_loop(2, patches, gather_step, 0)
    absorb_step(patches - 1)

    query_load.wait()
    queries = jnp.dot(
        scaled_rms(gathered[...]).astype(jnp.bfloat16),
        w_query[...],
        preferred_element_type=jnp.float32,
    ).astype(jnp.bfloat16)
    scale = 1.0 / math.sqrt(C)
    group = min(KEY_BLOCK // CELLS, patches)
    frame_cells = HALO // FD
    share_cells = SHARE // FD

    def fold(block, carry, f):
        run_max, run_total, run_acc = carry
        first = block * group
        pair = keyvals[pl.ds(first, group)].reshape(group * CELLS, 2 * C)
        codes = keys_ref[pl.ds(first, group)]
        allow = (codes // (RD * W)) % FD == f
        bias = jnp.where(allow, 0.0, -1e30)
        bias = jnp.concatenate([bias[j] for j in range(group)], axis=-1)
        scores = lax.dot_general(
            queries[f * share_cells : (f + 1) * share_cells],
            pair[:, :C],
            (((1,), (1,)), ((), ())),
            preferred_element_type=jnp.float32,
        )
        scores = scores * scale + bias
        top = jnp.max(scores, axis=-1, keepdims=True)
        if run_max is not None:
            top = jnp.maximum(top, run_max)
        powers = jnp.exp(scores - top)
        sums = jnp.sum(powers, axis=-1, keepdims=True)
        acc = jnp.dot(
            powers.astype(jnp.bfloat16), pair[:, C:], preferred_element_type=jnp.float32
        )
        if run_max is not None:
            factor = jnp.exp(run_max - top)
            sums = run_total * factor + sums
            acc = run_acc * factor + acc
        return top, sums, acc

    line = lax.broadcasted_iota(jnp.int32, (share_cells, 1), 0)

    def share_at(f, side):
        return pl.ds(pl.multiple_of(f * frame_cells + side * share_cells, share_cells), share_cells)

    def send_mixed(f, side):
        return pltpu.make_async_remote_copy(
            mixed.at[share_at(f, side)],
            mixed.at[share_at(f, side)],
            mixed_send.at[f],
            mixed_recv.at[f],
            device_id={"chan": other},
            device_id_type=MESH,
        )

    def attend(f):
        carry = fold(0, (None, None, None), f)
        if patches > group:
            carry = lax.fori_loop(
                1, patches // group, functools.partial(fold, f=f), carry
            )
        _, sums, acc = carry
        features = gathered[f * share_cells : (f + 1) * share_cells]
        mixed[share_at(f, core)] = (features + acc * (1.0 / sums)).astype(jnp.bfloat16)
        send_mixed(f, core).start()

    def activate(f, side):
        here = share_at(f, side)
        line_row = z * RD - 1 + side * rows_share + line // W
        inside = (line_row >= 0) & (line_row < patches * RD)
        v = scaled_rms(mixed[here].astype(jnp.float32))
        act = jnp.where(inside, (0.5 * v) * (1.0 + jnp.tanh(0.5 * v)), 0.0)
        before = jnp.where(line % W == 0, 0.0, pltpu.roll(act, 1, 0))
        after = jnp.where(line % W == W - 1, 0.0, pltpu.roll(act, share_cells - 1, 0))
        shifted3[here, 0:C] = before.astype(jnp.bfloat16)
        shifted3[here, C : 2 * C] = act.astype(jnp.bfloat16)
        shifted3[here, 2 * C : 3 * C] = after.astype(jnp.bfloat16)

    def conv_time(f, a):
        result = None
        for b in range(3):
            at_tap = 3 * (3 * a + b)
            weights = jnp.concatenate([conv[at_tap + c] for c in range(3)], axis=-1)
            first = f * frame_cells + b * W
            term = lax.dot_general(
                shifted3[first : first + band],
                weights,
                (((1,), (1,)), ((), ())),
                preferred_element_type=jnp.float32,
            )
            result = term if result is None else result + term
        return result

    def send_span(t):
        return pltpu.make_async_remote_copy(
            ahead.at[t],
            behind.at[t],
            span_send.at[t],
            span_recv.at[t],
            device_id={"span": x + 1},
            device_id_type=MESH,
        )

    width = out_ref.shape[-1]
    pick_from = lax.broadcasted_iota(jnp.int32, (C, width), 0)
    pick_to = lax.broadcasted_iota(jnp.int32, (C, width), 1) + core * width
    picks = jnp.where(pick_from == pick_to, 1.0, 0.0).astype(jnp.bfloat16)

    def own_mixed(f):
        first = f * frame_cells + W
        return jnp.dot(
            mixed[first : first + band], picks, preferred_element_type=jnp.float32
        )

    attend(1)
    activate(1, core)
    attend(0)
    activate(0, core)
    conv_load.wait()
    send_mixed(1, other).wait_recv()
    activate(1, other)
    ahead[1] = conv_time(1, 0).astype(jnp.bfloat16)
    when(has_after, lambda: send_span(1).start())
    middle = conv_time(1, 1)
    send_mixed(0, other).wait_recv()
    activate(0, other)
    ahead[0] = (conv_time(0, 0) + middle).astype(jnp.bfloat16)
    when(has_after, lambda: send_span(0).start())
    total[0:band] = conv_time(0, 2) + own_mixed(0)
    total[band : 2 * band] = conv_time(0, 1) + conv_time(1, 2) + own_mixed(1)

    @pl.when(x == 0)
    def _():
        out_ref[...] = total[...].astype(jnp.bfloat16)

    @pl.when(has_before)
    def _():
        for t in range(FD):
            send_span(t).wait_recv()
            here = slice(t * band, (t + 1) * band)
            out_ref[here] = (total[here] + behind[t].astype(jnp.float32)).astype(jnp.bfloat16)

    @pl.when(has_after)
    def _():
        for t in range(FD):
            send_span(t).wait_send()

    def finish(step, carry):
        for k in range(PIECES):

            def left_origin():
                when(has_right, lambda: send_right(z - step, k).wait_send())
                when(step > 0, lambda: send_pair(z - step, core, k).wait_send())

            def right_origin():
                when(has_left, lambda: send_left(z + step, k).wait_send())
                when(step > 0, lambda: send_pair(z + step, core, k).wait_send())

            when(z - step >= 0, left_origin)
            when(z + step < patches, right_origin)
        return carry

    lax.fori_loop(0, patches, finish, 0)
    for f in range(FD):
        send_mixed(f, core).wait_send()


def local(latent_tiles, route, w_query, w_keyval, conv_weight):
    patches = lax.axis_size("patch")
    spans = lax.axis_size("span")
    width = conv_weight.shape[-1]
    tiles_here, tile_cells = latent_tiles.shape[1:3]
    bf16, f32 = jnp.bfloat16, jnp.float32
    dma = pltpu.SemaphoreType.DMA
    anywhere = pl.BlockSpec(memory_space=pl.ANY)
    vmem = pl.BlockSpec(memory_space=pltpu.VMEM)
    result = pl.pallas_call(
        functools.partial(block_kernel, patches, spans),
        out_shape=pltpu.VMEM((FD * RD * W, width), bf16),
        in_specs=[anywhere] * 5,
        out_specs=vmem,
        scratch_shapes=[
            pltpu.VMEM((tiles_here, tile_cells, C), bf16),
            pltpu.VMEM(route.shape, jnp.int32),
            pltpu.VMEM((patches, 1, CELLS), jnp.int32),
            pltpu.VMEM((patches, CELLS, C), bf16),
            pltpu.VMEM((patches, CELLS, 2 * C), bf16),
            pltpu.VMEM((SHARE, C), f32),
            pltpu.VMEM((HALO, 3 * C), bf16),
            pltpu.VMEM((HALO, C), bf16),
            pltpu.VMEM((FD * RD * W, width), f32),
            pltpu.VMEM((C, C), bf16),
            pltpu.VMEM((C, 2 * C), bf16),
            pltpu.VMEM((27, width, C), bf16),
            pltpu.VMEM((FD, RD * W, width), bf16),
            pltpu.VMEM((FD, RD * W, width), bf16),
            dma((5,)),
            dma((patches, PIECES)),
            dma((patches, PIECES)),
            dma((patches, PIECES)),
            dma((patches, PIECES)),
            dma((patches, PIECES)),
            dma((patches, PIECES)),
            dma((FD,)),
            dma((FD,)),
            dma((FD,)),
            dma((FD,)),
        ],
        compiler_params=pltpu.CompilerParams(
            collective_id=0, has_side_effects=True, vmem_limit_bytes=56 * 1024 * 1024
        ),
    )(
        latent_tiles.reshape(tiles_here, tile_cells, C),
        route,
        w_query,
        w_keyval,
        conv_weight.transpose(0, 1, 2, 4, 3).reshape(27, width, C),
    )
    return result.reshape(FD, RD, W, width)


def solution(mesh):
    placed = (
        P(("clips", "span"), "patch", None, None),
        P(("clips", "span"), None),
        P(),
        P(),
        P(None, None, None, None, "chan"),
    )
    return jax.shard_map(
        local,
        mesh=mesh,
        in_specs=placed,
        out_specs=P(("clips", "span"), "patch", None, "chan"),
        check_vma=False,
    )
```

```python
import functools
import math

import jax
import jax.numpy as jnp
from jax import lax
from jax.experimental import pallas as pl
from jax.experimental.pallas import tpu as pltpu
from jax.sharding import PartitionSpec as P

C = 384
W = 64
RD = 2
FD = 2
CELLS = FD * RD * W
HALO = FD * (RD + 2) * W
SHARE = HALO // 2
PIECES = 2
KEY_BLOCK = 1024

epsilon = 1e-06
MESH = pl.DeviceIdType.MESH


def scaled_rms(wide):
    return wide * (1.0 / jnp.sqrt(jnp.mean(wide * wide, axis=-1, keepdims=True) + epsilon))


def block_kernel(
    patches,
    spans,
    tiles_ref,
    route_ref,
    w_query_ref,
    w_keyval_ref,
    conv_ref,
    out_ref,
    raw,
    places_of,
    keys_ref,
    tiles,
    keyvals,
    gathered,
    shifted3,
    mixed,
    total,
    w_query,
    w_keyval,
    conv,
    ahead,
    behind,
    load_sem,
    right_send,
    right_recv,
    left_send,
    left_recv,
    pair_send,
    pair_recv,
    span_send,
    span_recv,
    mixed_send,
    mixed_recv,
):
    z = lax.axis_index("patch")
    x = lax.axis_index("span")
    core = lax.axis_index("chan")
    other = 1 - core
    half = CELLS // 2
    piece = half // PIECES
    band = RD * W

    barrier = pltpu.get_barrier_semaphore()
    here, tile_cells = raw.shape[0], raw.shape[1]

    def greet(near, target):
        @pl.when(near)
        def _():
            pl.semaphore_signal(barrier, inc=1, device_id=target, device_id_type=MESH)

    has_left, has_right = z > 0, z < patches - 1
    has_before, has_after = x > 0, x < spans - 1
    greet(has_left, {"patch": z - 1})
    greet(has_right, {"patch": z + 1})
    greet(has_before, {"span": x - 1})
    greet(has_after, {"span": x + 1})
    pl.semaphore_signal(barrier, inc=1, device_id={"chan": other}, device_id_type=MESH)

    own_load = pltpu.make_async_copy(tiles_ref, raw, load_sem.at[0])
    own_load.start()
    keyval_load = pltpu.make_async_copy(w_keyval_ref, w_keyval, load_sem.at[1])
    keyval_load.start()
    route_load = pltpu.make_async_copy(route_ref, places_of, load_sem.at[4])
    route_load.start()
    query_load = pltpu.make_async_copy(w_query_ref, w_query, load_sem.at[2])
    query_load.start()
    conv_loads = [
        pltpu.make_async_copy(
            conv_ref.at[pl.ds(9 * a, 9)], conv.at[pl.ds(9 * a, 9)], load_sem.at[5 + a]
        )
        for a in range(3)
    ]
    for load in conv_loads:
        load.start()

    near_count = (
        1
        + jnp.where(has_left, 1, 0)
        + jnp.where(has_right, 1, 0)
        + jnp.where(has_before, 1, 0)
        + jnp.where(has_after, 1, 0)
    )
    own_load.wait()
    tiles[z] = raw[...].reshape(CELLS, C)
    pl.semaphore_wait(barrier, near_count)

    def part(origin, side, k):
        return tiles.at[origin, pl.ds(pl.multiple_of(side * half + k * piece, piece), piece)]

    def send_right(origin, k):
        return pltpu.make_async_remote_copy(
            part(origin, core, k),
            part(origin, core, k),
            right_send.at[origin, k],
            right_recv.at[origin, k],
            device_id={"patch": z + 1},
            device_id_type=MESH,
        )

    def send_left(origin, k):
        return pltpu.make_async_remote_copy(
            part(origin, core, k),
            part(origin, core, k),
            left_send.at[origin, k],
            left_recv.at[origin, k],
            device_id={"patch": z - 1},
            device_id_type=MESH,
        )

    def send_pair(origin, side, k):
        return pltpu.make_async_remote_copy(
            part(origin, side, k),
            part(origin, side, k),
            pair_send.at[origin, k],
            pair_recv.at[origin, k],
            device_id={"chan": other},
            device_id_type=MESH,
        )

    def when(condition, action):
        @pl.when(condition)
        def _():
            action()

    for k in range(PIECES):
        when(has_right, lambda: send_right(z, k).start())
        when(has_left, lambda: send_left(z, k).start())

    rows_share = (RD + 2) // 2
    at = lax.broadcasted_iota(jnp.int32, (SHARE, 1), 0)
    frame = at // (rows_share * W)
    row = z * RD - 1 + core * rows_share + (at // W) % rows_share
    owner = (row + RD) // RD - 1
    wanted = owner * CELLS + (frame * RD + (row + RD) % RD) * W + at % W

    def absorb(origin):
        values = tiles[origin]
        normed = scaled_rms(values.astype(jnp.float32)).astype(jnp.bfloat16)
        keyvals[origin] = jnp.dot(
            normed, w_keyval[...], preferred_element_type=jnp.float32
        ).astype(jnp.bfloat16)
        picks = jnp.where(keys_ref[origin] == wanted, 1.0, 0.0).astype(jnp.bfloat16)
        gathered[...] += jnp.dot(picks, values, preferred_element_type=jnp.float32)

    lanes = 2 * here
    spread_from = lax.broadcasted_iota(jnp.int32, (lanes, 2 * CELLS), 0)
    spread_to = lax.broadcasted_iota(jnp.int32, (lanes, 2 * CELLS), 1)
    spread = jnp.where(spread_to // tile_cells == spread_from, 1.0, 0.0).astype(jnp.bfloat16)
    cell = lax.broadcasted_iota(jnp.int32, (1, 2 * CELLS), 1) % tile_cells
    route_load.wait()
    for j in range(patches // 2):
        places = places_of[:, j * lanes : (j + 1) * lanes]
        digits = jnp.concatenate(
            [jnp.broadcast_to(d, (8, lanes)) for d in (places // 256, places % 256)], axis=0
        )
        wide = jnp.dot(
            digits.astype(jnp.float32).astype(jnp.bfloat16),
            spread,
            preferred_element_type=jnp.float32,
        )
        place = (wide[0:1] * 256.0 + wide[8:9]).astype(jnp.int32)
        codes = place * tile_cells + cell
        keys_ref[2 * j] = codes[:, :CELLS]
        keys_ref[2 * j + 1] = codes[:, CELLS:]

    gathered[...] = jnp.zeros_like(gathered)
    keyval_load.wait()
    absorb(z)

    def absorb_step(step):
        def from_pair(origin):
            for k in range(PIECES):
                send_pair(origin, other, k).wait_recv()
            absorb(origin)

        when(z - step >= 0, lambda: from_pair(z - step))
        when(z + step < patches, lambda: from_pair(z + step))

    def pass_on(step):
        for k in range(PIECES):

            def from_left():
                origin = z - step
                send_right(origin, k).wait_recv()
                when(has_right, lambda: send_right(origin, k).start())
                send_pair(origin, core, k).start()

            def from_right():
                origin = z + step
                send_left(origin, k).wait_recv()
                when(has_left, lambda: send_left(origin, k).start())
                send_pair(origin, core, k).start()

            when(z - step >= 0, from_left)
            when(z + step < patches, from_right)

    pass_on(1)
    inner = has_left & has_right

    def gather_step(step, carry):
        when(jnp.logical_not(inner), lambda: absorb_step(step - 1))
        pass_on(step)
        when(inner, lambda: absorb_step(step - 1))
        return carry

    lax.fori_loop(2, patches, gather_step, 0)
    absorb_step(patches - 1)

    query_load.wait()
    queries = jnp.dot(
        scaled_rms(gathered[...]).astype(jnp.bfloat16),
        w_query[...],
        preferred_element_type=jnp.float32,
    ).astype(jnp.bfloat16)
    scale = 1.0 / math.sqrt(C)
    group = min(KEY_BLOCK // CELLS, patches)
    frame_cells = HALO // FD
    share_cells = SHARE // FD

    def fold(block, carry):
        run_max, run_total, run_acc = carry
        first = block * group
        pair = keyvals[pl.ds(first, group)].reshape(group * CELLS, 2 * C)
        codes = keys_ref[pl.ds(first, group)]
        code_frame = (codes // (RD * W)) % FD
        raw_scores = lax.dot_general(
            queries, pair[:, :C], (((1,), (1,)), ((), ())), preferred_element_type=jnp.float32
        )
        parts = []
        for f in range(FD):
            bias = jnp.where(code_frame == f, 0.0, -1e30)
            bias = jnp.concatenate([bias[j] for j in range(group)], axis=-1)
            parts.append(raw_scores[f * share_cells : (f + 1) * share_cells] * scale + bias)
        scores = jnp.concatenate(parts, axis=0)
        top = jnp.max(scores, axis=-1, keepdims=True)
        if run_max is not None:
            top = jnp.maximum(top, run_max)
        powers = jnp.exp(scores - top)
        sums = jnp.sum(powers, axis=-1, keepdims=True)
        acc = jnp.dot(
            powers.astype(jnp.bfloat16), pair[:, C:], preferred_element_type=jnp.float32
        )
        if run_max is not None:
            factor = jnp.exp(run_max - top)
            sums = run_total * factor + sums
            acc = run_acc * factor + acc
        return top, sums, acc

    line = lax.broadcasted_iota(jnp.int32, (share_cells, 1), 0)

    def share_at(f, side):
        return pl.ds(pl.multiple_of(f * frame_cells + side * share_cells, share_cells), share_cells)

    def send_mixed(f, side):
        return pltpu.make_async_remote_copy(
            mixed.at[share_at(f, side)],
            mixed.at[share_at(f, side)],
            mixed_send.at[f],
            mixed_recv.at[f],
            device_id={"chan": other},
            device_id_type=MESH,
        )

    def attend():
        carry = fold(0, (None, None, None))
        if patches > group:
            carry = lax.fori_loop(1, patches // group, fold, carry)
        _, sums, acc = carry
        rounded = (gathered[...] + acc * (1.0 / sums)).astype(jnp.bfloat16)
        for f in range(FD):
            mixed[share_at(f, core)] = rounded[f * share_cells : (f + 1) * share_cells]
            send_mixed(f, core).start()

    def activate(f, side):
        here = share_at(f, side)
        line_row = z * RD - 1 + side * rows_share + line // W
        inside = (line_row >= 0) & (line_row < patches * RD)
        v = scaled_rms(mixed[here].astype(jnp.float32))
        act = jnp.where(inside, (0.5 * v) * (1.0 + jnp.tanh(0.5 * v)), 0.0)
        before = jnp.where(line % W == 0, 0.0, pltpu.roll(act, 1, 0))
        after = jnp.where(line % W == W - 1, 0.0, pltpu.roll(act, share_cells - 1, 0))
        shifted3[here, 0:C] = before.astype(jnp.bfloat16)
        shifted3[here, C : 2 * C] = act.astype(jnp.bfloat16)
        shifted3[here, 2 * C : 3 * C] = after.astype(jnp.bfloat16)

    def conv_times(times):
        result = None
        for b in range(3):
            weights = jnp.concatenate(
                [
                    jnp.concatenate([conv[3 * (3 * a + b) + c] for c in range(3)], axis=-1)
                    for a in times
                ],
                axis=0,
            )
            firsts = [f * frame_cells + b * W for f in range(FD)]
            cells = jnp.concatenate([shifted3[i : i + band] for i in firsts], axis=0)
            term = lax.dot_general(
                weights, cells, (((1,), (1,)), ((), ())), preferred_element_type=jnp.float32
            )
            result = term if result is None else result + term
        return result

    def send_span(t):
        return pltpu.make_async_remote_copy(
            ahead.at[t],
            behind.at[t],
            span_send.at[t],
            span_recv.at[t],
            device_id={"span": x + 1},
            device_id_type=MESH,
        )

    width = out_ref.shape[-1]
    pick_from = lax.broadcasted_iota(jnp.int32, (C, width), 0)
    pick_to = lax.broadcasted_iota(jnp.int32, (C, width), 1) + core * width
    picks = jnp.where(pick_from == pick_to, 1.0, 0.0).astype(jnp.bfloat16)

    def own_mixed(f):
        first = f * frame_cells + W
        return jnp.dot(
            mixed[first : first + band], picks, preferred_element_type=jnp.float32
        )

    attend()
    for f in range(FD):
        activate(f, core)
    for f in range(FD):
        send_mixed(f, other).wait_recv()
        activate(f, other)
    for load in conv_loads:
        load.wait()
    early = conv_times((0, 1))
    ahead[1] = early[:width, band:].astype(jnp.bfloat16)
    when(has_after, lambda: send_span(1).start())
    ahead[0] = (early[:width, :band] + early[width:, band:]).astype(jnp.bfloat16)
    when(has_after, lambda: send_span(0).start())
    late = conv_times((2,))
    total[0] = late[:, :band]
    total[1] = late[:, band:] + early[width:, :band]

    def finish(step, carry):
        for k in range(PIECES):

            def left_origin():
                when(has_right, lambda: send_right(z - step, k).wait_send())
                when(step > 0, lambda: send_pair(z - step, core, k).wait_send())

            def right_origin():
                when(has_left, lambda: send_left(z + step, k).wait_send())
                when(step > 0, lambda: send_pair(z + step, core, k).wait_send())

            when(z - step >= 0, left_origin)
            when(z + step < patches, right_origin)
        return carry

    lax.fori_loop(0, patches, finish, 0)
    for f in range(FD):
        send_mixed(f, core).wait_send()

    def write(t):
        here = slice(t * band, (t + 1) * band)
        out_ref[here] = (total[t].T + own_mixed(t)).astype(jnp.bfloat16)

    @pl.when(x == 0)
    def _():
        for t in range(FD):
            write(t)

    @pl.when(has_before)
    def _():
        for t in reversed(range(FD)):
            send_span(t).wait_recv()
            total[t] += behind[t].astype(jnp.float32)
            write(t)

    @pl.when(has_after)
    def _():
        for t in range(FD):
            send_span(t).wait_send()


def local(latent_tiles, route, w_query, w_keyval, conv_weight):
    patches = lax.axis_size("patch")
    spans = lax.axis_size("span")
    width = conv_weight.shape[-1]
    tiles_here, tile_cells = latent_tiles.shape[1:3]
    bf16, f32 = jnp.bfloat16, jnp.float32
    dma = pltpu.SemaphoreType.DMA
    anywhere = pl.BlockSpec(memory_space=pl.ANY)
    vmem = pl.BlockSpec(memory_space=pltpu.VMEM)
    result = pl.pallas_call(
        functools.partial(block_kernel, patches, spans),
        out_shape=pltpu.VMEM((FD * RD * W, width), bf16),
        in_specs=[anywhere] * 5,
        out_specs=vmem,
        scratch_shapes=[
            pltpu.VMEM((tiles_here, tile_cells, C), bf16),
            pltpu.VMEM(route.shape, jnp.int32),
            pltpu.VMEM((patches, 1, CELLS), jnp.int32),
            pltpu.VMEM((patches, CELLS, C), bf16),
            pltpu.VMEM((patches, CELLS, 2 * C), bf16),
            pltpu.VMEM((SHARE, C), f32),
            pltpu.VMEM((HALO, 3 * C), bf16),
            pltpu.VMEM((HALO, C), bf16),
            pltpu.VMEM((FD, width, RD * W), f32),
            pltpu.VMEM((C, C), bf16),
            pltpu.VMEM((C, 2 * C), bf16),
            pltpu.VMEM((27, width, C), bf16),
            pltpu.VMEM((FD, width, RD * W), bf16),
            pltpu.VMEM((FD, width, RD * W), bf16),
            dma((8,)),
            dma((patches, PIECES)),
            dma((patches, PIECES)),
            dma((patches, PIECES)),
            dma((patches, PIECES)),
            dma((patches, PIECES)),
            dma((patches, PIECES)),
            dma((FD,)),
            dma((FD,)),
            dma((FD,)),
            dma((FD,)),
        ],
        compiler_params=pltpu.CompilerParams(
            collective_id=0, has_side_effects=True, vmem_limit_bytes=56 * 1024 * 1024
        ),
    )(
        latent_tiles.reshape(tiles_here, tile_cells, C),
        route,
        w_query,
        w_keyval,
        conv_weight.transpose(0, 1, 2, 4, 3).reshape(27, width, C),
    )
    return result.reshape(FD, RD, W, width)


def solution(mesh):
    placed = (
        P(("clips", "span"), "patch", None, None),
        P(("clips", "span"), None),
        P(),
        P(),
        P(None, None, None, None, "chan"),
    )
    return jax.shard_map(
        local,
        mesh=mesh,
        in_specs=placed,
        out_specs=P(("clips", "span"), "patch", None, "chan"),
        check_vma=False,
    )
```

```python
import functools
import math

import jax
import jax.numpy as jnp
from jax import lax
from jax.experimental import pallas as pl
from jax.experimental.pallas import tpu as pltpu
from jax.sharding import PartitionSpec as P

C = 384
W = 64
RD = 2
FD = 2
CELLS = FD * RD * W
HALO = FD * (RD + 2) * W
SHARE = HALO // 2
PIECES = 2
KEY_BLOCK = 1024

epsilon = 1e-06
MESH = pl.DeviceIdType.MESH


def scaled_rms(wide):
    return wide * (1.0 / jnp.sqrt(jnp.mean(wide * wide, axis=-1, keepdims=True) + epsilon))


def block_kernel(
    patches,
    spans,
    tiles_ref,
    route_ref,
    w_query_ref,
    w_keyval_ref,
    conv_ref,
    out_ref,
    raw,
    places_of,
    keys_ref,
    tiles,
    keyvals,
    gathered,
    shifted3,
    mixed,
    total,
    w_query,
    w_keyval,
    conv,
    ahead,
    behind,
    load_sem,
    right_send,
    right_recv,
    left_send,
    left_recv,
    pair_send,
    pair_recv,
    span_send,
    span_recv,
    mixed_send,
    mixed_recv,
):
    z = lax.axis_index("patch")
    x = lax.axis_index("span")
    core = lax.axis_index("chan")
    other = 1 - core
    half = CELLS // 2
    piece = half // PIECES
    band = RD * W

    barrier = pltpu.get_barrier_semaphore()
    here, tile_cells = raw.shape[0], raw.shape[1]

    def greet(near, target):
        @pl.when(near)
        def _():
            pl.semaphore_signal(barrier, inc=1, device_id=target, device_id_type=MESH)

    has_left, has_right = z > 0, z < patches - 1
    has_before, has_after = x > 0, x < spans - 1
    greet(has_left, {"patch": z - 1})
    greet(has_right, {"patch": z + 1})
    greet(has_before, {"span": x - 1})
    greet(has_after, {"span": x + 1})
    pl.semaphore_signal(barrier, inc=1, device_id={"chan": other}, device_id_type=MESH)

    own_load = pltpu.make_async_copy(tiles_ref, raw, load_sem.at[0])
    own_load.start()
    keyval_load = pltpu.make_async_copy(w_keyval_ref, w_keyval, load_sem.at[1])
    keyval_load.start()
    route_load = pltpu.make_async_copy(route_ref, places_of, load_sem.at[4])
    route_load.start()
    query_load = pltpu.make_async_copy(w_query_ref, w_query, load_sem.at[2])
    query_load.start()
    conv_loads = [
        pltpu.make_async_copy(
            conv_ref.at[pl.ds(9 * a, 9)], conv.at[pl.ds(9 * a, 9)], load_sem.at[5 + a]
        )
        for a in range(3)
    ]
    for load in conv_loads:
        load.start()

    near_count = (
        1
        + jnp.where(has_left, 1, 0)
        + jnp.where(has_right, 1, 0)
        + jnp.where(has_before, 1, 0)
        + jnp.where(has_after, 1, 0)
    )
    own_load.wait()
    tiles[z] = raw[...].reshape(CELLS, C)
    pl.semaphore_wait(barrier, near_count)

    def part(origin, side, k):
        return tiles.at[origin, pl.ds(pl.multiple_of(side * half + k * piece, piece), piece)]

    def send_right(origin, k):
        return pltpu.make_async_remote_copy(
            part(origin, core, k),
            part(origin, core, k),
            right_send.at[origin, k],
            right_recv.at[origin, k],
            device_id={"patch": z + 1},
            device_id_type=MESH,
        )

    def send_left(origin, k):
        return pltpu.make_async_remote_copy(
            part(origin, core, k),
            part(origin, core, k),
            left_send.at[origin, k],
            left_recv.at[origin, k],
            device_id={"patch": z - 1},
            device_id_type=MESH,
        )

    def send_pair(origin, side, k):
        return pltpu.make_async_remote_copy(
            part(origin, side, k),
            part(origin, side, k),
            pair_send.at[origin, k],
            pair_recv.at[origin, k],
            device_id={"chan": other},
            device_id_type=MESH,
        )

    def when(condition, action):
        @pl.when(condition)
        def _():
            action()

    for k in range(PIECES):
        when(has_right, lambda: send_right(z, k).start())
        when(has_left, lambda: send_left(z, k).start())

    rows_share = (RD + 2) // 2
    at = lax.broadcasted_iota(jnp.int32, (SHARE, 1), 0)
    frame = at // (rows_share * W)
    row = z * RD - 1 + core * rows_share + (at // W) % rows_share
    owner = (row + RD) // RD - 1
    wanted = owner * CELLS + (frame * RD + (row + RD) % RD) * W + at % W

    def absorb(origin, rows):
        values = tiles[origin, rows]
        normed = scaled_rms(values.astype(jnp.float32)).astype(jnp.bfloat16)
        keyvals[origin, rows] = jnp.dot(
            normed, w_keyval[...], preferred_element_type=jnp.float32
        ).astype(jnp.bfloat16)
        picks = jnp.where(keys_ref[origin, :, rows] == wanted, 1.0, 0.0).astype(jnp.bfloat16)
        gathered[...] += jnp.dot(picks, values, preferred_element_type=jnp.float32)

    lanes = 2 * here
    spread_from = lax.broadcasted_iota(jnp.int32, (lanes, 2 * CELLS), 0)
    spread_to = lax.broadcasted_iota(jnp.int32, (lanes, 2 * CELLS), 1)
    spread = jnp.where(spread_to // tile_cells == spread_from, 1.0, 0.0).astype(jnp.bfloat16)
    cell = lax.broadcasted_iota(jnp.int32, (1, 2 * CELLS), 1) % tile_cells
    route_load.wait()
    for j in range(patches // 2):
        places = places_of[:, j * lanes : (j + 1) * lanes]
        digits = jnp.concatenate(
            [jnp.broadcast_to(d, (8, lanes)) for d in (places // 256, places % 256)], axis=0
        )
        wide = jnp.dot(
            digits.astype(jnp.float32).astype(jnp.bfloat16),
            spread,
            preferred_element_type=jnp.float32,
        )
        place = (wide[0:1] * 256.0 + wide[8:9]).astype(jnp.int32)
        codes = place * tile_cells + cell
        keys_ref[2 * j] = codes[:, :CELLS]
        keys_ref[2 * j + 1] = codes[:, CELLS:]

    gathered[...] = jnp.zeros_like(gathered)
    keyval_load.wait()
    absorb(z, pl.ds(0, CELLS))

    def absorb_step(step):
        def from_pair(origin):
            absorb(origin, pl.ds(pl.multiple_of(core * half, half), half))
            for k in range(PIECES):
                send_pair(origin, other, k).wait_recv()
            absorb(origin, pl.ds(pl.multiple_of(other * half, half), half))

        when(z - step >= 0, lambda: from_pair(z - step))
        when(z + step < patches, lambda: from_pair(z + step))

    def pass_on(step):
        for k in range(PIECES):

            def from_left():
                origin = z - step
                send_right(origin, k).wait_recv()
                when(has_right, lambda: send_right(origin, k).start())
                send_pair(origin, core, k).start()

            def from_right():
                origin = z + step
                send_left(origin, k).wait_recv()
                when(has_left, lambda: send_left(origin, k).start())
                send_pair(origin, core, k).start()

            when(z - step >= 0, from_left)
            when(z + step < patches, from_right)

    pass_on(1)
    inner = has_left & has_right

    def gather_step(step, carry):
        when(jnp.logical_not(inner), lambda: absorb_step(step - 1))
        pass_on(step)
        when(inner, lambda: absorb_step(step - 1))
        return carry

    lax.fori_loop(2, patches, gather_step, 0)
    absorb_step(patches - 1)

    query_load.wait()
    queries = jnp.dot(
        scaled_rms(gathered[...]).astype(jnp.bfloat16),
        w_query[...],
        preferred_element_type=jnp.float32,
    ).astype(jnp.bfloat16)
    scale = 1.0 / math.sqrt(C)
    group = min(KEY_BLOCK // CELLS, patches)
    frame_cells = HALO // FD
    share_cells = SHARE // FD

    def fold(block, carry):
        run_max, run_total, run_acc = carry
        first = block * group
        pair = keyvals[pl.ds(first, group)].reshape(group * CELLS, 2 * C)
        codes = keys_ref[pl.ds(first, group)]
        code_frame = (codes // (RD * W)) % FD
        raw_scores = lax.dot_general(
            queries, pair[:, :C], (((1,), (1,)), ((), ())), preferred_element_type=jnp.float32
        )
        parts = []
        for f in range(FD):
            bias = jnp.where(code_frame == f, 0.0, -1e30)
            bias = jnp.concatenate([bias[j] for j in range(group)], axis=-1)
            parts.append(raw_scores[f * share_cells : (f + 1) * share_cells] * scale + bias)
        scores = jnp.concatenate(parts, axis=0)
        top = jnp.max(scores, axis=-1, keepdims=True)
        if run_max is not None:
            top = jnp.maximum(top, run_max)
        powers = jnp.exp(scores - top)
        sums = jnp.sum(powers, axis=-1, keepdims=True)
        acc = jnp.dot(
            powers.astype(jnp.bfloat16), pair[:, C:], preferred_element_type=jnp.float32
        )
        if run_max is not None:
            factor = jnp.exp(run_max - top)
            sums = run_total * factor + sums
            acc = run_acc * factor + acc
        return top, sums, acc

    line = lax.broadcasted_iota(jnp.int32, (SHARE, 1), 0)

    def share_at(f, side):
        return pl.ds(pl.multiple_of(f * frame_cells + side * share_cells, share_cells), share_cells)

    def send_mixed(f, side):
        return pltpu.make_async_remote_copy(
            mixed.at[share_at(f, side)],
            mixed.at[share_at(f, side)],
            mixed_send.at[f],
            mixed_recv.at[f],
            device_id={"chan": other},
            device_id_type=MESH,
        )

    def attend():
        carry = fold(0, (None, None, None))
        if patches > group:
            carry = lax.fori_loop(1, patches // group, fold, carry)
        _, sums, acc = carry
        rounded = (gathered[...] + acc * (1.0 / sums)).astype(jnp.bfloat16)
        for f in range(FD):
            mixed[share_at(f, core)] = rounded[f * share_cells : (f + 1) * share_cells]
            send_mixed(f, core).start()

    def activate(side):
        line_row = z * RD - 1 + side * rows_share + (line // W) % rows_share
        inside = (line_row >= 0) & (line_row < patches * RD)
        held = jnp.concatenate([mixed[share_at(f, side)] for f in range(FD)], axis=0)
        v = scaled_rms(held.astype(jnp.float32))
        act = jnp.where(inside, (0.5 * v) * (1.0 + jnp.tanh(0.5 * v)), 0.0)
        before = jnp.where(line % W == 0, 0.0, pltpu.roll(act, 1, 0))
        after = jnp.where(line % W == W - 1, 0.0, pltpu.roll(act, SHARE - 1, 0))
        columns = jnp.concatenate([before, act, after], axis=-1).astype(jnp.bfloat16)
        for f in range(FD):
            shifted3[share_at(f, side)] = columns[f * share_cells : (f + 1) * share_cells]

    def conv_times(times):
        result = None
        for b in range(3):
            weights = jnp.concatenate(
                [
                    jnp.concatenate([conv[3 * (3 * a + b) + c] for c in range(3)], axis=-1)
                    for a in times
                ],
                axis=0,
            )
            firsts = [f * frame_cells + b * W for f in range(FD)]
            cells = jnp.concatenate([shifted3[i : i + band] for i in firsts], axis=0)
            term = lax.dot_general(
                weights, cells, (((1,), (1,)), ((), ())), preferred_element_type=jnp.float32
            )
            result = term if result is None else result + term
        return result

    def send_span(t):
        return pltpu.make_async_remote_copy(
            ahead.at[t],
            behind.at[t],
            span_send.at[t],
            span_recv.at[t],
            device_id={"span": x + 1},
            device_id_type=MESH,
        )

    width = out_ref.shape[-1]
    pick_from = lax.broadcasted_iota(jnp.int32, (C, width), 0)
    pick_to = lax.broadcasted_iota(jnp.int32, (C, width), 1) + core * width
    picks = jnp.where(pick_from == pick_to, 1.0, 0.0).astype(jnp.bfloat16)

    def own_mixed(f):
        first = f * frame_cells + W
        return jnp.dot(
            mixed[first : first + band], picks, preferred_element_type=jnp.float32
        )

    attend()
    activate(core)
    for f in range(FD):
        send_mixed(f, other).wait_recv()
    activate(other)
    for load in conv_loads:
        load.wait()
    oldest = conv_times((0,))
    ahead[1] = oldest[:, band:].astype(jnp.bfloat16)
    when(has_after, lambda: send_span(1).start())
    middle = conv_times((1,))
    ahead[0] = (oldest[:, :band] + middle[:, band:]).astype(jnp.bfloat16)
    when(has_after, lambda: send_span(0).start())
    late = conv_times((2,))
    total[0] = late[:, :band]
    total[1] = late[:, band:] + middle[:, :band]

    def finish(step, carry):
        for k in range(PIECES):

            def left_origin():
                when(has_right, lambda: send_right(z - step, k).wait_send())
                when(step > 0, lambda: send_pair(z - step, core, k).wait_send())

            def right_origin():
                when(has_left, lambda: send_left(z + step, k).wait_send())
                when(step > 0, lambda: send_pair(z + step, core, k).wait_send())

            when(z - step >= 0, left_origin)
            when(z + step < patches, right_origin)
        return carry

    lax.fori_loop(0, patches, finish, 0)
    for f in range(FD):
        send_mixed(f, core).wait_send()

    def write(t):
        here = slice(t * band, (t + 1) * band)
        out_ref[here] = (total[t].T + own_mixed(t)).astype(jnp.bfloat16)

    @pl.when(x == 0)
    def _():
        for t in range(FD):
            write(t)

    @pl.when(has_before)
    def _():
        for t in reversed(range(FD)):
            send_span(t).wait_recv()
            total[t] += behind[t].astype(jnp.float32)
            write(t)

    @pl.when(has_after)
    def _():
        for t in range(FD):
            send_span(t).wait_send()


def local(latent_tiles, route, w_query, w_keyval, conv_weight):
    patches = lax.axis_size("patch")
    spans = lax.axis_size("span")
    width = conv_weight.shape[-1]
    tiles_here, tile_cells = latent_tiles.shape[1:3]
    bf16, f32 = jnp.bfloat16, jnp.float32
    dma = pltpu.SemaphoreType.DMA
    anywhere = pl.BlockSpec(memory_space=pl.ANY)
    vmem = pl.BlockSpec(memory_space=pltpu.VMEM)
    result = pl.pallas_call(
        functools.partial(block_kernel, patches, spans),
        out_shape=pltpu.VMEM((FD * RD * W, width), bf16),
        in_specs=[anywhere] * 5,
        out_specs=vmem,
        scratch_shapes=[
            pltpu.VMEM((tiles_here, tile_cells, C), bf16),
            pltpu.VMEM(route.shape, jnp.int32),
            pltpu.VMEM((patches, 1, CELLS), jnp.int32),
            pltpu.VMEM((patches, CELLS, C), bf16),
            pltpu.VMEM((patches, CELLS, 2 * C), bf16),
            pltpu.VMEM((SHARE, C), f32),
            pltpu.VMEM((HALO, 3 * C), bf16),
            pltpu.VMEM((HALO, C), bf16),
            pltpu.VMEM((FD, width, RD * W), f32),
            pltpu.VMEM((C, C), bf16),
            pltpu.VMEM((C, 2 * C), bf16),
            pltpu.VMEM((27, width, C), bf16),
            pltpu.VMEM((FD, width, RD * W), bf16),
            pltpu.VMEM((FD, width, RD * W), bf16),
            dma((8,)),
            dma((patches, PIECES)),
            dma((patches, PIECES)),
            dma((patches, PIECES)),
            dma((patches, PIECES)),
            dma((patches, PIECES)),
            dma((patches, PIECES)),
            dma((FD,)),
            dma((FD,)),
            dma((FD,)),
            dma((FD,)),
        ],
        compiler_params=pltpu.CompilerParams(
            collective_id=0, has_side_effects=True, vmem_limit_bytes=56 * 1024 * 1024
        ),
    )(
        latent_tiles.reshape(tiles_here, tile_cells, C),
        route,
        w_query,
        w_keyval,
        conv_weight.transpose(0, 1, 2, 4, 3).reshape(27, width, C),
    )
    return result.reshape(FD, RD, W, width)


def solution(mesh):
    placed = (
        P(("clips", "span"), "patch", None, None),
        P(("clips", "span"), None),
        P(),
        P(),
        P(None, None, None, None, "chan"),
    )
    return jax.shard_map(
        local,
        mesh=mesh,
        in_specs=placed,
        out_specs=P(("clips", "span"), "patch", None, "chan"),
        check_vma=False,
    )
```

```python
import functools
import math

import jax
import jax.numpy as jnp
from jax import lax
from jax.experimental import pallas as pl
from jax.experimental.pallas import tpu as pltpu
from jax.sharding import PartitionSpec as P

C = 384
W = 64
RD = 2
FD = 2
CELLS = FD * RD * W
HALO = FD * (RD + 2) * W
SHARE = HALO // 2
PIECES = 2
KEY_BLOCK = 1024

epsilon = 1e-06
MESH = pl.DeviceIdType.MESH


def scaled_rms(wide):
    return wide * lax.rsqrt(jnp.mean(wide * wide, axis=-1, keepdims=True) + epsilon)


def block_kernel(
    patches,
    spans,
    tiles_ref,
    route_ref,
    w_query_ref,
    w_keyval_ref,
    conv_ref,
    out_ref,
    raw,
    places_of,
    keys_ref,
    tiles,
    keyvals,
    gathered,
    shifted3,
    mixed,
    total,
    w_query,
    w_keyval,
    conv,
    ahead,
    behind,
    load_sem,
    right_send,
    right_recv,
    left_send,
    left_recv,
    pair_send,
    pair_recv,
    span_send,
    span_recv,
    mixed_send,
    mixed_recv,
):
    z = lax.axis_index("patch")
    x = lax.axis_index("span")
    core = lax.axis_index("chan")
    other = 1 - core
    half = CELLS // 2
    piece = half // PIECES
    band = RD * W

    barrier = pltpu.get_barrier_semaphore()
    here, tile_cells = raw.shape[0], raw.shape[1]

    def greet(near, target):
        @pl.when(near)
        def _():
            pl.semaphore_signal(barrier, inc=1, device_id=target, device_id_type=MESH)

    has_left, has_right = z > 0, z < patches - 1
    has_before, has_after = x > 0, x < spans - 1
    greet(has_left, {"patch": z - 1})
    greet(has_right, {"patch": z + 1})
    greet(has_before, {"span": x - 1})
    greet(has_after, {"span": x + 1})
    pl.semaphore_signal(barrier, inc=1, device_id={"chan": other}, device_id_type=MESH)

    own_load = pltpu.make_async_copy(tiles_ref, raw, load_sem.at[0])
    own_load.start()
    keyval_load = pltpu.make_async_copy(w_keyval_ref, w_keyval, load_sem.at[1])
    keyval_load.start()
    route_load = pltpu.make_async_copy(route_ref, places_of, load_sem.at[4])
    route_load.start()
    query_load = pltpu.make_async_copy(w_query_ref, w_query, load_sem.at[2])
    query_load.start()
    conv_loads = [
        pltpu.make_async_copy(
            conv_ref.at[pl.ds(9 * a, 9)], conv.at[pl.ds(9 * a, 9)], load_sem.at[5 + a]
        )
        for a in range(3)
    ]
    for load in conv_loads:
        load.start()

    near_count = (
        1
        + jnp.where(has_left, 1, 0)
        + jnp.where(has_right, 1, 0)
        + jnp.where(has_before, 1, 0)
        + jnp.where(has_after, 1, 0)
    )
    own_load.wait()
    tiles[z] = raw[...].reshape(CELLS, C)
    pl.semaphore_wait(barrier, near_count)

    def part(origin, side, k):
        return tiles.at[origin, pl.ds(pl.multiple_of(side * half + k * piece, piece), piece)]

    def send_right(origin, k):
        return pltpu.make_async_remote_copy(
            part(origin, core, k),
            part(origin, core, k),
            right_send.at[origin, k],
            right_recv.at[origin, k],
            device_id={"patch": z + 1},
            device_id_type=MESH,
        )

    def send_left(origin, k):
        return pltpu.make_async_remote_copy(
            part(origin, core, k),
            part(origin, core, k),
            left_send.at[origin, k],
            left_recv.at[origin, k],
            device_id={"patch": z - 1},
            device_id_type=MESH,
        )

    def send_pair(origin, side, k):
        return pltpu.make_async_remote_copy(
            part(origin, side, k),
            part(origin, side, k),
            pair_send.at[origin, k],
            pair_recv.at[origin, k],
            device_id={"chan": other},
            device_id_type=MESH,
        )

    def when(condition, action):
        @pl.when(condition)
        def _():
            action()

    for k in range(PIECES):
        when(has_right, lambda: send_right(z, k).start())
        when(has_left, lambda: send_left(z, k).start())

    rows_share = (RD + 2) // 2
    at = lax.broadcasted_iota(jnp.int32, (SHARE, 1), 0)
    frame = at // (rows_share * W)
    row = z * RD - 1 + core * rows_share + (at // W) % rows_share
    owner = (row + RD) // RD - 1
    wanted = owner * CELLS + (frame * RD + (row + RD) % RD) * W + at % W

    def absorb(origin):
        values = tiles[origin]
        normed = scaled_rms(values.astype(jnp.float32)).astype(jnp.bfloat16)
        keyvals[origin] = jnp.dot(
            normed, w_keyval[...], preferred_element_type=jnp.float32
        ).astype(jnp.bfloat16)
        picks = jnp.where(keys_ref[origin] == wanted, 1.0, 0.0).astype(jnp.bfloat16)
        gathered[...] += jnp.dot(picks, values, preferred_element_type=jnp.float32)

    lanes = 2 * here
    spread_from = lax.broadcasted_iota(jnp.int32, (lanes, 2 * CELLS), 0)
    spread_to = lax.broadcasted_iota(jnp.int32, (lanes, 2 * CELLS), 1)
    spread = jnp.where(spread_to // tile_cells == spread_from, 1.0, 0.0).astype(jnp.bfloat16)
    cell = lax.broadcasted_iota(jnp.int32, (1, 2 * CELLS), 1) % tile_cells
    route_load.wait()
    for j in range(patches // 2):
        places = places_of[:, j * lanes : (j + 1) * lanes]
        digits = jnp.concatenate(
            [jnp.broadcast_to(d, (8, lanes)) for d in (places // 256, places % 256)], axis=0
        )
        wide = jnp.dot(
            digits.astype(jnp.float32).astype(jnp.bfloat16),
            spread,
            preferred_element_type=jnp.float32,
        )
        place = (wide[0:1] * 256.0 + wide[8:9]).astype(jnp.int32)
        codes = place * tile_cells + cell
        keys_ref[2 * j] = codes[:, :CELLS]
        keys_ref[2 * j + 1] = codes[:, CELLS:]

    gathered[...] = jnp.zeros_like(gathered)
    keyval_load.wait()
    absorb(z)

    def absorb_step(step):
        def from_pair(origin):
            for k in range(PIECES):
                send_pair(origin, other, k).wait_recv()
            absorb(origin)

        when(z - step >= 0, lambda: from_pair(z - step))
        when(z + step < patches, lambda: from_pair(z + step))

    def pass_on(step):
        for k in range(PIECES):

            def from_left():
                origin = z - step
                send_right(origin, k).wait_recv()
                when(has_right, lambda: send_right(origin, k).start())
                send_pair(origin, core, k).start()

            def from_right():
                origin = z + step
                send_left(origin, k).wait_recv()
                when(has_left, lambda: send_left(origin, k).start())
                send_pair(origin, core, k).start()

            when(z - step >= 0, from_left)
            when(z + step < patches, from_right)

    pass_on(1)
    inner = has_left & has_right

    def gather_step(step, carry):
        when(jnp.logical_not(inner), lambda: absorb_step(step - 1))
        pass_on(step)
        when(inner, lambda: absorb_step(step - 1))
        return carry

    lax.fori_loop(2, patches, gather_step, 0)
    absorb_step(patches - 1)

    query_load.wait()
    queries = jnp.dot(
        scaled_rms(gathered[...]).astype(jnp.bfloat16),
        w_query[...],
        preferred_element_type=jnp.float32,
    ).astype(jnp.bfloat16)
    scale = 1.0 / math.sqrt(C)
    group = min(KEY_BLOCK // CELLS, patches)
    frame_cells = HALO // FD
    share_cells = SHARE // FD

    def fold(block, carry):
        run_max, run_total, run_acc = carry
        first = block * group
        pair = keyvals[pl.ds(first, group)].reshape(group * CELLS, 2 * C)
        codes = keys_ref[pl.ds(first, group)]
        code_frame = (codes // (RD * W)) % FD
        raw_scores = lax.dot_general(
            queries, pair[:, :C], (((1,), (1,)), ((), ())), preferred_element_type=jnp.float32
        )
        parts = []
        for f in range(FD):
            bias = jnp.where(code_frame == f, 0.0, -1e30)
            bias = jnp.concatenate([bias[j] for j in range(group)], axis=-1)
            parts.append(raw_scores[f * share_cells : (f + 1) * share_cells] * scale + bias)
        scores = jnp.concatenate(parts, axis=0)
        top = jnp.max(scores, axis=-1, keepdims=True)
        if run_max is not None:
            top = jnp.maximum(top, run_max)
        powers = jnp.exp(scores - top)
        sums = jnp.sum(powers, axis=-1, keepdims=True)
        acc = jnp.dot(
            powers.astype(jnp.bfloat16), pair[:, C:], preferred_element_type=jnp.float32
        )
        if run_max is not None:
            factor = jnp.exp(run_max - top)
            sums = run_total * factor + sums
            acc = run_acc * factor + acc
        return top, sums, acc

    line = lax.broadcasted_iota(jnp.int32, (share_cells, 1), 0)

    def share_at(f, side):
        return pl.ds(pl.multiple_of(f * frame_cells + side * share_cells, share_cells), share_cells)

    def send_mixed(f, side):
        return pltpu.make_async_remote_copy(
            mixed.at[share_at(f, side)],
            mixed.at[share_at(f, side)],
            mixed_send.at[f],
            mixed_recv.at[f],
            device_id={"chan": other},
            device_id_type=MESH,
        )

    def attend():
        carry = fold(0, (None, None, None))
        if patches > group:
            carry = lax.fori_loop(1, patches // group, fold, carry)
        _, sums, acc = carry
        rounded = (gathered[...] + acc * (1.0 / sums)).astype(jnp.bfloat16)
        for f in range(FD):
            mixed[share_at(f, core)] = rounded[f * share_cells : (f + 1) * share_cells]
            send_mixed(f, core).start()

    def activate(f, side):
        here = share_at(f, side)
        line_row = z * RD - 1 + side * rows_share + line // W
        inside = (line_row >= 0) & (line_row < patches * RD)
        v = scaled_rms(mixed[here].astype(jnp.float32))
        act = jnp.where(inside, (0.5 * v) * (1.0 + jnp.tanh(0.5 * v)), 0.0)
        before = jnp.where(line % W == 0, 0.0, pltpu.roll(act, 1, 0))
        after = jnp.where(line % W == W - 1, 0.0, pltpu.roll(act, share_cells - 1, 0))
        shifted3[here, 0:C] = before.astype(jnp.bfloat16)
        shifted3[here, C : 2 * C] = act.astype(jnp.bfloat16)
        shifted3[here, 2 * C : 3 * C] = after.astype(jnp.bfloat16)

    def conv_times(times):
        result = None
        for b in range(3):
            weights = jnp.concatenate(
                [
                    jnp.concatenate([conv[3 * (3 * a + b) + c] for c in range(3)], axis=-1)
                    for a in times
                ],
                axis=0,
            )
            firsts = [f * frame_cells + b * W for f in range(FD)]
            cells = jnp.concatenate([shifted3[i : i + band] for i in firsts], axis=0)
            term = lax.dot_general(
                weights, cells, (((1,), (1,)), ((), ())), preferred_element_type=jnp.float32
            )
            result = term if result is None else result + term
        return result

    def send_span(t):
        return pltpu.make_async_remote_copy(
            ahead.at[t],
            behind.at[t],
            span_send.at[t],
            span_recv.at[t],
            device_id={"span": x + 1},
            device_id_type=MESH,
        )

    width = out_ref.shape[-1]
    pick_from = lax.broadcasted_iota(jnp.int32, (C, width), 0)
    pick_to = lax.broadcasted_iota(jnp.int32, (C, width), 1) + core * width
    picks = jnp.where(pick_from == pick_to, 1.0, 0.0).astype(jnp.bfloat16)

    def own_mixed(f):
        first = f * frame_cells + W
        return jnp.dot(
            mixed[first : first + band], picks, preferred_element_type=jnp.float32
        )

    attend()
    for f in range(FD):
        activate(f, core)
    for f in range(FD):
        send_mixed(f, other).wait_recv()
        activate(f, other)
    for load in conv_loads:
        load.wait()
    oldest = conv_times((0,))
    ahead[1] = oldest[:, band:].astype(jnp.bfloat16)
    when(has_after, lambda: send_span(1).start())
    middle = conv_times((1,))
    ahead[0] = (oldest[:, :band] + middle[:, band:]).astype(jnp.bfloat16)
    when(has_after, lambda: send_span(0).start())
    late = conv_times((2,))
    total[0] = late[:, :band]
    total[1] = late[:, band:] + middle[:, :band]

    def finish(step, carry):
        for k in range(PIECES):

            def left_origin():
                when(has_right, lambda: send_right(z - step, k).wait_send())
                when(step > 0, lambda: send_pair(z - step, core, k).wait_send())

            def right_origin():
                when(has_left, lambda: send_left(z + step, k).wait_send())
                when(step > 0, lambda: send_pair(z + step, core, k).wait_send())

            when(z - step >= 0, left_origin)
            when(z + step < patches, right_origin)
        return carry

    lax.fori_loop(0, patches, finish, 0)
    for f in range(FD):
        send_mixed(f, core).wait_send()

    def write(t):
        here = slice(t * band, (t + 1) * band)
        out_ref[here] = (total[t].T + own_mixed(t)).astype(jnp.bfloat16)

    @pl.when(x == 0)
    def _():
        for t in range(FD):
            write(t)

    @pl.when(has_before)
    def _():
        for t in reversed(range(FD)):
            send_span(t).wait_recv()
            total[t] += behind[t].astype(jnp.float32)
            write(t)

    @pl.when(has_after)
    def _():
        for t in range(FD):
            send_span(t).wait_send()


def local(latent_tiles, route, w_query, w_keyval, conv_weight):
    patches = lax.axis_size("patch")
    spans = lax.axis_size("span")
    width = conv_weight.shape[-1]
    tiles_here, tile_cells = latent_tiles.shape[1:3]
    bf16, f32 = jnp.bfloat16, jnp.float32
    dma = pltpu.SemaphoreType.DMA
    anywhere = pl.BlockSpec(memory_space=pl.ANY)
    vmem = pl.BlockSpec(memory_space=pltpu.VMEM)
    result = pl.pallas_call(
        functools.partial(block_kernel, patches, spans),
        out_shape=pltpu.VMEM((FD * RD * W, width), bf16),
        in_specs=[anywhere] * 5,
        out_specs=vmem,
        scratch_shapes=[
            pltpu.VMEM((tiles_here, tile_cells, C), bf16),
            pltpu.VMEM(route.shape, jnp.int32),
            pltpu.VMEM((patches, 1, CELLS), jnp.int32),
            pltpu.VMEM((patches, CELLS, C), bf16),
            pltpu.VMEM((patches, CELLS, 2 * C), bf16),
            pltpu.VMEM((SHARE, C), f32),
            pltpu.VMEM((HALO, 3 * C), bf16),
            pltpu.VMEM((HALO, C), bf16),
            pltpu.VMEM((FD, width, RD * W), f32),
            pltpu.VMEM((C, C), bf16),
            pltpu.VMEM((C, 2 * C), bf16),
            pltpu.VMEM((27, width, C), bf16),
            pltpu.VMEM((FD, width, RD * W), bf16),
            pltpu.VMEM((FD, width, RD * W), bf16),
            dma((8,)),
            dma((patches, PIECES)),
            dma((patches, PIECES)),
            dma((patches, PIECES)),
            dma((patches, PIECES)),
            dma((patches, PIECES)),
            dma((patches, PIECES)),
            dma((FD,)),
            dma((FD,)),
            dma((FD,)),
            dma((FD,)),
        ],
        compiler_params=pltpu.CompilerParams(
            collective_id=0, has_side_effects=True, vmem_limit_bytes=56 * 1024 * 1024
        ),
    )(
        latent_tiles.reshape(tiles_here, tile_cells, C),
        route,
        w_query,
        w_keyval,
        conv_weight.transpose(0, 1, 2, 4, 3).reshape(27, width, C),
    )
    return result.reshape(FD, RD, W, width)


def solution(mesh):
    placed = (
        P(("clips", "span"), "patch", None, None),
        P(("clips", "span"), None),
        P(),
        P(),
        P(None, None, None, None, "chan"),
    )
    return jax.shard_map(
        local,
        mesh=mesh,
        in_specs=placed,
        out_specs=P(("clips", "span"), "patch", None, "chan"),
        check_vma=False,
    )
```

```python
import functools
import math

import jax
import jax.numpy as jnp
from jax import lax
from jax.experimental import pallas as pl
from jax.experimental.pallas import tpu as pltpu
from jax.sharding import PartitionSpec as P

C = 384
W = 64
RD = 2
FD = 2
CELLS = FD * RD * W
HALO = FD * (RD + 2) * W
SHARE = HALO // 2
PIECES = 2
KEY_BLOCK = 1024

epsilon = 1e-06
MESH = pl.DeviceIdType.MESH


def scaled_rms(wide):
    return wide * (1.0 / jnp.sqrt(jnp.mean(wide * wide, axis=-1, keepdims=True) + epsilon))


def block_kernel(
    patches,
    spans,
    tiles_ref,
    route_ref,
    w_query_ref,
    w_keyval_ref,
    conv_ref,
    out_ref,
    raw,
    places_of,
    keys_ref,
    tiles,
    keyvals,
    gathered,
    shifted3,
    mixed,
    total,
    w_query,
    w_keyval,
    conv,
    ahead,
    behind,
    load_sem,
    right_send,
    right_recv,
    left_send,
    left_recv,
    pair_send,
    pair_recv,
    span_send,
    span_recv,
    mixed_send,
    mixed_recv,
    keyval_send,
    keyval_recv,
):
    z = lax.axis_index("patch")
    x = lax.axis_index("span")
    core = lax.axis_index("chan")
    other = 1 - core
    half = CELLS // 2
    piece = half // PIECES
    band = RD * W

    barrier = pltpu.get_barrier_semaphore()
    here, tile_cells = raw.shape[0], raw.shape[1]

    def greet(near, target):
        @pl.when(near)
        def _():
            pl.semaphore_signal(barrier, inc=1, device_id=target, device_id_type=MESH)

    has_left, has_right = z > 0, z < patches - 1
    has_before, has_after = x > 0, x < spans - 1
    greet(has_left, {"patch": z - 1})
    greet(has_right, {"patch": z + 1})
    greet(has_before, {"span": x - 1})
    greet(has_after, {"span": x + 1})
    pl.semaphore_signal(barrier, inc=1, device_id={"chan": other}, device_id_type=MESH)

    own_load = pltpu.make_async_copy(tiles_ref, raw, load_sem.at[0])
    own_load.start()
    keyval_load = pltpu.make_async_copy(w_keyval_ref, w_keyval, load_sem.at[1])
    keyval_load.start()
    route_load = pltpu.make_async_copy(route_ref, places_of, load_sem.at[4])
    route_load.start()
    query_load = pltpu.make_async_copy(w_query_ref, w_query, load_sem.at[2])
    query_load.start()
    conv_loads = [
        pltpu.make_async_copy(
            conv_ref.at[pl.ds(9 * a, 9)], conv.at[pl.ds(9 * a, 9)], load_sem.at[5 + a]
        )
        for a in range(3)
    ]
    for load in conv_loads:
        load.start()

    near_count = (
        1
        + jnp.where(has_left, 1, 0)
        + jnp.where(has_right, 1, 0)
        + jnp.where(has_before, 1, 0)
        + jnp.where(has_after, 1, 0)
    )
    own_load.wait()
    tiles[z] = raw[...].reshape(CELLS, C)
    pl.semaphore_wait(barrier, near_count)

    def part(origin, side, k):
        return tiles.at[origin, pl.ds(pl.multiple_of(side * half + k * piece, piece), piece)]

    def send_right(origin, k):
        return pltpu.make_async_remote_copy(
            part(origin, core, k),
            part(origin, core, k),
            right_send.at[origin, k],
            right_recv.at[origin, k],
            device_id={"patch": z + 1},
            device_id_type=MESH,
        )

    def send_left(origin, k):
        return pltpu.make_async_remote_copy(
            part(origin, core, k),
            part(origin, core, k),
            left_send.at[origin, k],
            left_recv.at[origin, k],
            device_id={"patch": z - 1},
            device_id_type=MESH,
        )

    def send_pair(origin, side, k):
        return pltpu.make_async_remote_copy(
            part(origin, side, k),
            part(origin, side, k),
            pair_send.at[origin, k],
            pair_recv.at[origin, k],
            device_id={"chan": other},
            device_id_type=MESH,
        )

    def when(condition, action):
        @pl.when(condition)
        def _():
            action()

    for k in range(PIECES):
        when(has_right, lambda: send_right(z, k).start())
        when(has_left, lambda: send_left(z, k).start())

    rows_share = (RD + 2) // 2
    at = lax.broadcasted_iota(jnp.int32, (SHARE, 1), 0)
    frame = at // (rows_share * W)
    row = z * RD - 1 + core * rows_share + (at // W) % rows_share
    owner = (row + RD) // RD - 1
    wanted = owner * CELLS + (frame * RD + (row + RD) % RD) * W + at % W

    def project(origin, rows):
        normed = scaled_rms(tiles[origin, rows].astype(jnp.float32)).astype(jnp.bfloat16)
        keyvals[origin, rows] = jnp.dot(
            normed, w_keyval[...], preferred_element_type=jnp.float32
        ).astype(jnp.bfloat16)

    def pick(origin):
        picks = jnp.where(keys_ref[origin] == wanted, 1.0, 0.0).astype(jnp.bfloat16)
        gathered[...] += jnp.dot(picks, tiles[origin], preferred_element_type=jnp.float32)

    def send_keyvals(origin, side):
        rows = pl.ds(pl.multiple_of(side * half, half), half)
        return pltpu.make_async_remote_copy(
            keyvals.at[origin, rows],
            keyvals.at[origin, rows],
            keyval_send.at[origin],
            keyval_recv.at[origin],
            device_id={"chan": other},
            device_id_type=MESH,
        )

    lanes = 2 * here
    spread_from = lax.broadcasted_iota(jnp.int32, (lanes, 2 * CELLS), 0)
    spread_to = lax.broadcasted_iota(jnp.int32, (lanes, 2 * CELLS), 1)
    spread = jnp.where(spread_to // tile_cells == spread_from, 1.0, 0.0).astype(jnp.bfloat16)
    cell = lax.broadcasted_iota(jnp.int32, (1, 2 * CELLS), 1) % tile_cells
    route_load.wait()
    for j in range(patches // 2):
        places = places_of[:, j * lanes : (j + 1) * lanes]
        digits = jnp.concatenate(
            [jnp.broadcast_to(d, (8, lanes)) for d in (places // 256, places % 256)], axis=0
        )
        wide = jnp.dot(
            digits.astype(jnp.float32).astype(jnp.bfloat16),
            spread,
            preferred_element_type=jnp.float32,
        )
        place = (wide[0:1] * 256.0 + wide[8:9]).astype(jnp.int32)
        codes = place * tile_cells + cell
        keys_ref[2 * j] = codes[:, :CELLS]
        keys_ref[2 * j + 1] = codes[:, CELLS:]

    gathered[...] = jnp.zeros_like(gathered)
    keyval_load.wait()
    project(z, pl.ds(0, CELLS))
    pick(z)

    def absorb_step(step):
        def from_pair(origin):
            project(origin, pl.ds(pl.multiple_of(core * half, half), half))
            send_keyvals(origin, core).start()
            for k in range(PIECES):
                send_pair(origin, other, k).wait_recv()
            pick(origin)

        when(z - step >= 0, lambda: from_pair(z - step))
        when(z + step < patches, lambda: from_pair(z + step))

    def pass_on(step):
        for k in range(PIECES):

            def from_left():
                origin = z - step
                send_right(origin, k).wait_recv()
                when(has_right, lambda: send_right(origin, k).start())
                send_pair(origin, core, k).start()

            def from_right():
                origin = z + step
                send_left(origin, k).wait_recv()
                when(has_left, lambda: send_left(origin, k).start())
                send_pair(origin, core, k).start()

            when(z - step >= 0, from_left)
            when(z + step < patches, from_right)

    pass_on(1)
    inner = has_left & has_right

    def gather_step(step, carry):
        when(jnp.logical_not(inner), lambda: absorb_step(step - 1))
        pass_on(step)
        when(inner, lambda: absorb_step(step - 1))
        return carry

    lax.fori_loop(2, patches, gather_step, 0)
    absorb_step(patches - 1)

    def keyvals_here(step, carry):
        when(z - step >= 0, lambda: send_keyvals(z - step, other).wait_recv())
        when(z + step < patches, lambda: send_keyvals(z + step, other).wait_recv())
        return carry

    def keyvals_gone(step, carry):
        when(z - step >= 0, lambda: send_keyvals(z - step, core).wait_send())
        when(z + step < patches, lambda: send_keyvals(z + step, core).wait_send())
        return carry

    query_load.wait()
    queries = jnp.dot(
        scaled_rms(gathered[...]).astype(jnp.bfloat16),
        w_query[...],
        preferred_element_type=jnp.float32,
    ).astype(jnp.bfloat16)
    scale = 1.0 / math.sqrt(C)
    group = min(KEY_BLOCK // CELLS, patches)
    frame_cells = HALO // FD
    share_cells = SHARE // FD

    def fold(block, carry):
        run_max, run_total, run_acc = carry
        first = block * group
        pair = keyvals[pl.ds(first, group)].reshape(group * CELLS, 2 * C)
        codes = keys_ref[pl.ds(first, group)]
        code_frame = (codes // (RD * W)) % FD
        raw_scores = lax.dot_general(
            queries, pair[:, :C], (((1,), (1,)), ((), ())), preferred_element_type=jnp.float32
        )
        parts = []
        for f in range(FD):
            bias = jnp.where(code_frame == f, 0.0, -1e30)
            bias = jnp.concatenate([bias[j] for j in range(group)], axis=-1)
            parts.append(raw_scores[f * share_cells : (f + 1) * share_cells] * scale + bias)
        scores = jnp.concatenate(parts, axis=0)
        top = jnp.max(scores, axis=-1, keepdims=True)
        if run_max is not None:
            top = jnp.maximum(top, run_max)
        powers = jnp.exp(scores - top)
        sums = jnp.sum(powers, axis=-1, keepdims=True)
        acc = jnp.dot(
            powers.astype(jnp.bfloat16), pair[:, C:], preferred_element_type=jnp.float32
        )
        if run_max is not None:
            factor = jnp.exp(run_max - top)
            sums = run_total * factor + sums
            acc = run_acc * factor + acc
        return top, sums, acc

    line = lax.broadcasted_iota(jnp.int32, (share_cells, 1), 0)

    def share_at(f, side):
        return pl.ds(pl.multiple_of(f * frame_cells + side * share_cells, share_cells), share_cells)

    def send_mixed(f, side):
        return pltpu.make_async_remote_copy(
            mixed.at[share_at(f, side)],
            mixed.at[share_at(f, side)],
            mixed_send.at[f],
            mixed_recv.at[f],
            device_id={"chan": other},
            device_id_type=MESH,
        )

    def attend():
        carry = fold(0, (None, None, None))
        if patches > group:
            carry = lax.fori_loop(1, patches // group, fold, carry)
        _, sums, acc = carry
        rounded = (gathered[...] + acc * (1.0 / sums)).astype(jnp.bfloat16)
        for f in range(FD):
            mixed[share_at(f, core)] = rounded[f * share_cells : (f + 1) * share_cells]
            send_mixed(f, core).start()

    def activate(f, side):
        here = share_at(f, side)
        line_row = z * RD - 1 + side * rows_share + line // W
        inside = (line_row >= 0) & (line_row < patches * RD)
        v = scaled_rms(mixed[here].astype(jnp.float32))
        act = jnp.where(inside, (0.5 * v) * (1.0 + jnp.tanh(0.5 * v)), 0.0)
        before = jnp.where(line % W == 0, 0.0, pltpu.roll(act, 1, 0))
        after = jnp.where(line % W == W - 1, 0.0, pltpu.roll(act, share_cells - 1, 0))
        shifted3[here, 0:C] = before.astype(jnp.bfloat16)
        shifted3[here, C : 2 * C] = act.astype(jnp.bfloat16)
        shifted3[here, 2 * C : 3 * C] = after.astype(jnp.bfloat16)

    def conv_times(times):
        result = None
        for b in range(3):
            weights = jnp.concatenate(
                [
                    jnp.concatenate([conv[3 * (3 * a + b) + c] for c in range(3)], axis=-1)
                    for a in times
                ],
                axis=0,
            )
            firsts = [f * frame_cells + b * W for f in range(FD)]
            cells = jnp.concatenate([shifted3[i : i + band] for i in firsts], axis=0)
            term = lax.dot_general(
                weights, cells, (((1,), (1,)), ((), ())), preferred_element_type=jnp.float32
            )
            result = term if result is None else result + term
        return result

    def send_span(t):
        return pltpu.make_async_remote_copy(
            ahead.at[t],
            behind.at[t],
            span_send.at[t],
            span_recv.at[t],
            device_id={"span": x + 1},
            device_id_type=MESH,
        )

    width = out_ref.shape[-1]
    pick_from = lax.broadcasted_iota(jnp.int32, (C, width), 0)
    pick_to = lax.broadcasted_iota(jnp.int32, (C, width), 1) + core * width
    picks = jnp.where(pick_from == pick_to, 1.0, 0.0).astype(jnp.bfloat16)

    def own_mixed(f):
        first = f * frame_cells + W
        return jnp.dot(
            mixed[first : first + band], picks, preferred_element_type=jnp.float32
        )

    lax.fori_loop(1, patches, keyvals_here, 0)
    attend()
    for f in range(FD):
        activate(f, core)
    for f in range(FD):
        send_mixed(f, other).wait_recv()
        activate(f, other)
    for load in conv_loads:
        load.wait()
    early = conv_times((0, 1))
    ahead[1] = early[:width, band:].astype(jnp.bfloat16)
    when(has_after, lambda: send_span(1).start())
    ahead[0] = (early[:width, :band] + early[width:, band:]).astype(jnp.bfloat16)
    when(has_after, lambda: send_span(0).start())
    late = conv_times((2,))
    total[0] = late[:, :band]
    total[1] = late[:, band:] + early[width:, :band]

    def finish(step, carry):
        for k in range(PIECES):

            def left_origin():
                when(has_right, lambda: send_right(z - step, k).wait_send())
                when(step > 0, lambda: send_pair(z - step, core, k).wait_send())

            def right_origin():
                when(has_left, lambda: send_left(z + step, k).wait_send())
                when(step > 0, lambda: send_pair(z + step, core, k).wait_send())

            when(z - step >= 0, left_origin)
            when(z + step < patches, right_origin)
        return carry

    lax.fori_loop(0, patches, finish, 0)
    lax.fori_loop(1, patches, keyvals_gone, 0)
    for f in range(FD):
        send_mixed(f, core).wait_send()

    def write(t):
        here = slice(t * band, (t + 1) * band)
        out_ref[here] = (total[t].T + own_mixed(t)).astype(jnp.bfloat16)

    @pl.when(x == 0)
    def _():
        for t in range(FD):
            write(t)

    @pl.when(has_before)
    def _():
        for t in reversed(range(FD)):
            send_span(t).wait_recv()
            total[t] += behind[t].astype(jnp.float32)
            write(t)

    @pl.when(has_after)
    def _():
        for t in range(FD):
            send_span(t).wait_send()


def local(latent_tiles, route, w_query, w_keyval, conv_weight):
    patches = lax.axis_size("patch")
    spans = lax.axis_size("span")
    width = conv_weight.shape[-1]
    tiles_here, tile_cells = latent_tiles.shape[1:3]
    bf16, f32 = jnp.bfloat16, jnp.float32
    dma = pltpu.SemaphoreType.DMA
    anywhere = pl.BlockSpec(memory_space=pl.ANY)
    vmem = pl.BlockSpec(memory_space=pltpu.VMEM)
    result = pl.pallas_call(
        functools.partial(block_kernel, patches, spans),
        out_shape=pltpu.VMEM((FD * RD * W, width), bf16),
        in_specs=[anywhere] * 5,
        out_specs=vmem,
        scratch_shapes=[
            pltpu.VMEM((tiles_here, tile_cells, C), bf16),
            pltpu.VMEM(route.shape, jnp.int32),
            pltpu.VMEM((patches, 1, CELLS), jnp.int32),
            pltpu.VMEM((patches, CELLS, C), bf16),
            pltpu.VMEM((patches, CELLS, 2 * C), bf16),
            pltpu.VMEM((SHARE, C), f32),
            pltpu.VMEM((HALO, 3 * C), bf16),
            pltpu.VMEM((HALO, C), bf16),
            pltpu.VMEM((FD, width, RD * W), f32),
            pltpu.VMEM((C, C), bf16),
            pltpu.VMEM((C, 2 * C), bf16),
            pltpu.VMEM((27, width, C), bf16),
            pltpu.VMEM((FD, width, RD * W), bf16),
            pltpu.VMEM((FD, width, RD * W), bf16),
            dma((8,)),
            dma((patches, PIECES)),
            dma((patches, PIECES)),
            dma((patches, PIECES)),
            dma((patches, PIECES)),
            dma((patches, PIECES)),
            dma((patches, PIECES)),
            dma((FD,)),
            dma((FD,)),
            dma((FD,)),
            dma((FD,)),
            dma((patches,)),
            dma((patches,)),
        ],
        compiler_params=pltpu.CompilerParams(
            collective_id=0, has_side_effects=True, vmem_limit_bytes=56 * 1024 * 1024
        ),
    )(
        latent_tiles.reshape(tiles_here, tile_cells, C),
        route,
        w_query,
        w_keyval,
        conv_weight.transpose(0, 1, 2, 4, 3).reshape(27, width, C),
    )
    return result.reshape(FD, RD, W, width)


def solution(mesh):
    placed = (
        P(("clips", "span"), "patch", None, None),
        P(("clips", "span"), None),
        P(),
        P(),
        P(None, None, None, None, "chan"),
    )
    return jax.shard_map(
        local,
        mesh=mesh,
        in_specs=placed,
        out_specs=P(("clips", "span"), "patch", None, "chan"),
        check_vma=False,
    )
```
